512 devices in a mesh: row: 64 (over z, y), chan: 8 (over x, core).
Axes of the slice: x: 4, y: 8, z: 8, core: 2. Of those that a mesh axis runs over, the one named last changes fastest.
Arguments:
- pair: bfloat16 [1024, 1024, 128], P('row'), may hold values from -6 to 6
- ln_gain: float32 [128], replicated, may hold values from 0.25 to 1.75
- ln_bias: float32 [128], replicated, may hold values from -3 to 3
- w_a_gate: bfloat16 [128, 128], P(None, 'chan'), may hold values from -0.5 to 0.5
- w_a_proj: bfloat16 [128, 128], P(None, 'chan'), may hold values from -0.5 to 0.5
- w_b_gate: bfloat16 [128, 128], P(None, 'chan'), may hold values from -0.5 to 0.5
- w_b_proj: bfloat16 [128, 128], P(None, 'chan'), may hold values from -0.5 to 0.5
- w_gate: bfloat16 [128, 128], replicated, may hold values from -0.5 to 0.5
- out_gain: float32 [128], replicated, may hold values from 0.25 to 1.75
- out_bias: float32 [128], replicated, may hold values from -3 to 3
- w_out: bfloat16 [128, 128], replicated, may hold values from -0.5 to 0.5
Outputs:
- update: bfloat16 [1024, 1024, 128], P('row', 'chan')
The draws below stay inside these ranges and needn't reach their ends.
All inputs are finite; a program needn't handle non-finite values.
Results may differ from the reference program's by a relative error of at most 0.014.
Values may be sent and summed in bfloat16 or wider, within the bound.
No kernel may reach another device: no remote copies, remote signals or barrier semaphores. Data moves between devices by JAX's collectives and lax.ppermute only.
A program may use at most 128 MiB of HBM per device.

```python
import jax
import jax.numpy as jnp
from jax import lax

CP = 128
CH = 128
N = 1024


def block_levels(key, extent, pieces, low, largest):
    gain, own = 1.0, jax.random.fold_in(key, 6)
    for axis_at, shards_of in pieces:
        heights = jnp.exp(jax.random.uniform(jax.random.fold_in(own, axis_at), (shards_of,), jnp.float32, low / len(pieces), largest / len(pieces)))
        gain = gain * jnp.repeat(heights, extent[axis_at] // shards_of).reshape([-1 if axis == axis_at else 1 for axis in range(len(extent))])
    return gain


def normal_values(own_key, dims, scale, bound, cuts=(), dtype=jnp.bfloat16):
    gain = block_levels(own_key, dims, cuts, -0.22, 0.18) if cuts else 1.0
    drawn = jax.random.normal(own_key, dims, jnp.float32) * scale * gain
    return jnp.minimum(jnp.maximum(drawn, -bound), bound).astype(dtype)


def setup_inputs(seed: int = 0) -> dict:
    splits = jax.random.split(jax.random.key(seed), 12)
    return {
        "pair": normal_values(splits[0], (N, N, CP), 1.0, 6.0, ((0, 64),)),
        "ln_gain": jnp.clip(1.0 + 0.15 * jax.random.normal(splits[1], (CP,), jnp.float32), 0.25, 1.75),
        "ln_bias": normal_values(splits[2], (CP,), 0.5, 3.0, (), jnp.float32),
        "w_a_gate": normal_values(splits[3], (CP, CH), CP ** -0.5, 0.5, ((1, 8),)),
        "w_a_proj": normal_values(splits[4], (CP, CH), CP ** -0.5, 0.5, ((1, 8),)),
        "w_b_gate": normal_values(splits[5], (CP, CH), CP ** -0.5, 0.5, ((1, 8),)),
        "w_b_proj": normal_values(splits[6], (CP, CH), CP ** -0.5, 0.5, ((1, 8),)),
        "w_gate": normal_values(splits[7], (CP, CP), CP ** -0.5, 0.5),
        "out_gain": jnp.clip(1.0 + 0.15 * jax.random.normal(splits[8], (CH,), jnp.float32), 0.25, 1.75),
        "out_bias": normal_values(splits[9], (CH,), 0.5, 3.0, (), jnp.float32),
        "w_out": normal_values(splits[10], (CH, CP), CH ** -0.5, 0.5),
    }


def reference(pair, ln_gain, ln_bias, w_a_gate, w_a_proj, w_b_gate, w_b_proj, w_gate, out_gain, out_bias, w_out):
    values = pair.astype(jnp.float32)
    mean = lax.optimization_barrier(jnp.mean(values, axis=-1, keepdims=True))
    var = lax.optimization_barrier(jnp.mean((values - mean) ** 2, axis=-1, keepdims=True))
    normed = ((values - mean) * jax.lax.rsqrt(var + 1e-05) * ln_gain + ln_bias).astype(jnp.bfloat16)
    flat = normed.reshape(N * N, CP)

    def project(w_g, w_p):
        g = jnp.dot(flat, w_g, preferred_element_type=jnp.float32)
        p = jnp.dot(flat, w_p, preferred_element_type=jnp.float32)
        return (jax.nn.sigmoid(g) * p).astype(jnp.bfloat16).reshape(N, N, CH).transpose(2, 0, 1)
    left = project(w_a_gate, w_a_proj)
    right = project(w_b_gate, w_b_proj)
    mixed = jnp.einsum('cki,ckj->cij', left.astype(jnp.float32), right.astype(jnp.float32))
    mu = lax.optimization_barrier(jnp.mean(mixed, axis=0, keepdims=True))
    sigma = lax.optimization_barrier(jnp.mean((mixed - mu) ** 2, axis=0, keepdims=True))
    scaled = ((mixed - mu) * jax.lax.rsqrt(sigma + 1e-05) * out_gain[:, None, None] + out_bias[:, None, None]).astype(jnp.bfloat16)
    flat_scaled = scaled.reshape(CH, N * N)
    proj = jax.lax.dot_general(flat_scaled, w_out, (((0,), (0,)), ((), ())), preferred_element_type=jnp.float32)
    gate = jax.nn.sigmoid(jnp.dot(flat, w_gate, preferred_element_type=jnp.float32))
    return (proj * gate).astype(jnp.bfloat16).reshape(N, N, CP)
```

```python
import jax
import jax.numpy as jnp
from jax import lax
from jax.experimental import pallas as pl
from jax.experimental.pallas import tpu as pltpu
from jax.sharding import Mesh
from jax.sharding import PartitionSpec as P

F32 = jnp.float32
BF16 = jnp.bfloat16
VMEM_LIMIT = 48 * 1024 * 1024
EPS = 1e-05


def params():
    return pltpu.CompilerParams(vmem_limit_bytes=VMEM_LIMIT)


def norm_kernel(pos, pair, gain, bias, out):
    values = pair[...].astype(F32)
    mean = jnp.mean(values, axis=-1, keepdims=True)
    centred = values - mean
    var = jnp.mean(centred * centred, axis=-1, keepdims=True)
    out[...] = (centred * lax.rsqrt(var + EPS) * gain[...] + bias[...]).astype(BF16)


def norm_columns(pos, pair, gain, bias, width):
    rows, _, chans = pair.shape
    step = rows // 4
    return pl.pallas_call(
        norm_kernel,
        out_shape=jax.ShapeDtypeStruct((rows, width, chans), BF16),
        grid_spec=pltpu.PrefetchScalarGridSpec(
            num_scalar_prefetch=1,
            grid=(4,),
            in_specs=[
                pl.BlockSpec((step, width, chans), lambda s, pos: (s, pos[0], 0)),
                pl.BlockSpec((1, 1, chans), lambda s, pos: (0, 0, 0)),
                pl.BlockSpec((1, 1, chans), lambda s, pos: (0, 0, 0)),
            ],
            out_specs=pl.BlockSpec((step, width, chans), lambda s, pos: (s, 0, 0)),
        ),
        compiler_params=params(),
        cost_estimate=pl.CostEstimate(
            flops=8 * rows * width * chans, bytes_accessed=4 * rows * width * chans, transcendentals=rows * width
        ),
    )(pos, pair, gain.reshape(1, 1, chans), bias.reshape(1, 1, chans))


def project_kernel(normed, weights, out):
    rows, width, chans = normed.shape
    slab = weights.shape[0] // 2
    flat = normed[...].reshape(rows * width, chans)
    both = lax.dot_general(weights[...], flat, (((1,), (1,)), ((), ())), preferred_element_type=F32)
    value = jax.nn.sigmoid(both[:slab]) * both[slab:]
    parts = [value[:, k * width : (k + 1) * width] for k in range(rows)]
    out[...] = jnp.swapaxes(jnp.stack(parts, axis=0), 0, 1).astype(BF16)


def project(normed, weights):
    rows, width, chans = normed.shape
    slab = weights.shape[0] // 2
    lanes = 128
    return pl.pallas_call(
        project_kernel,
        out_shape=jax.ShapeDtypeStruct((slab, rows, width), BF16),
        grid=(width // lanes,),
        in_specs=[
            pl.BlockSpec((rows, lanes, chans), lambda s: (0, s, 0)),
            pl.BlockSpec((2 * slab, chans), lambda s: (0, 0)),
        ],
        out_specs=pl.BlockSpec((slab, rows, lanes), lambda s: (0, 0, s)),
        compiler_params=params(),
        cost_estimate=pl.CostEstimate(
            flops=4 * rows * width * slab * chans,
            bytes_accessed=2 * rows * width * (slab + chans),
            transcendentals=rows * width * slab,
        ),
    )(normed, weights)


def gate_kernel(pos, normed, weights, out):
    rows, width, chans = normed.shape
    flat = normed[...].reshape(rows * width, chans)
    got = jnp.dot(flat, weights[...], preferred_element_type=F32)
    out[...] = jax.nn.sigmoid(got).reshape(rows, width, chans)


def output_gate(pos, normed, weights, width):
    rows, _, chans = normed.shape
    step = rows // 2
    return pl.pallas_call(
        gate_kernel,
        out_shape=jax.ShapeDtypeStruct((rows, width, chans), F32),
        grid_spec=pltpu.PrefetchScalarGridSpec(
            num_scalar_prefetch=1,
            grid=(2,),
            in_specs=[
                pl.BlockSpec((step, width, chans), lambda s, pos: (s, pos[1], 0)),
                pl.BlockSpec((chans, chans), lambda s, pos: (0, 0)),
            ],
            out_specs=pl.BlockSpec((step, width, chans), lambda s, pos: (s, 0, 0)),
        ),
        compiler_params=params(),
        cost_estimate=pl.CostEstimate(
            flops=2 * rows * width * chans * chans,
            bytes_accessed=6 * rows * width * chans,
            transcendentals=rows * width * chans,
        ),
    )(pos, normed, weights)


def mix_kernel(pos, left, right, out):
    half = right.shape[1] // 2
    core = pos[1]
    block = left[0]
    for which in range(2):
        at = pl.multiple_of((core if which == 0 else 1 - core) * half, half)
        mixed = lax.dot_general(
            block, right[:, pl.ds(at, half)], (((0,), (0,)), ((), ())), preferred_element_type=F32
        )
        rows = out.shape[1] // 2
        out[:, which * rows : (which + 1) * rows, :] = mixed.reshape(out.shape[0], rows, half).astype(BF16)


def mix(pos, left, right, rows):
    slices, depth, height = left.shape
    width = right.shape[1]
    per = height // rows
    return pl.pallas_call(
        mix_kernel,
        out_shape=jax.ShapeDtypeStruct((slices * per, 2 * rows, width // 2), BF16),
        grid_spec=pltpu.PrefetchScalarGridSpec(
            num_scalar_prefetch=1,
            grid=(slices,),
            in_specs=[
                pl.BlockSpec((1, depth, height), lambda s, pos: (s, 0, 0)),
                pl.BlockSpec((depth, width), lambda s, pos: (0, 0)),
            ],
            out_specs=pl.BlockSpec((per, 2 * rows, width // 2), lambda s, pos: (s, 0, 0)),
        ),
        compiler_params=params(),
        cost_estimate=pl.CostEstimate(
            flops=2 * slices * depth * height * width,
            bytes_accessed=2 * (slices * depth * height + depth * width + slices * height * width),
            transcendentals=0,
        ),
    )(pos, left, right)


def finish_kernel(pos, own, other, gain, bias, weights, gate, out):
    core = pos[1]
    slab, rows, width = own.shape
    mine = own[...].astype(F32)
    theirs = other[...].astype(F32)
    total = 2 * slab
    mean = (jnp.sum(mine, axis=0) + jnp.sum(theirs, axis=0)) / total
    mine = mine - mean[None]
    theirs = theirs - mean[None]
    var = (jnp.sum(mine * mine, axis=0) + jnp.sum(theirs * theirs, axis=0)) / total
    scale = lax.rsqrt(var + EPS)
    mine = jnp.swapaxes(mine * scale[None], 0, 1)
    theirs = jnp.swapaxes(theirs * scale[None], 0, 1)
    mine = (mine * gain[core][None] + bias[core][None]).astype(BF16)
    theirs = (theirs * gain[1 - core][None] + bias[1 - core][None]).astype(BF16)
    contract = (((0,), (0,)), ((), ()))
    for row in range(rows):
        proj = lax.dot_general(mine[row], weights[core], contract, preferred_element_type=F32)
        proj = proj + lax.dot_general(theirs[row], weights[1 - core], contract, preferred_element_type=F32)
        out[row] = (proj * gate[row]).astype(BF16)


def finish(pos, mixed, other, gain, bias, weights, gate):
    slab, rows, width = other.shape
    outs = weights.shape[-1]
    whole = lambda *shape: pl.BlockSpec(shape, lambda s, pos: (0,) * len(shape))
    return pl.pallas_call(
        finish_kernel,
        out_shape=jax.ShapeDtypeStruct((rows, width, outs), BF16),
        grid_spec=pltpu.PrefetchScalarGridSpec(
            num_scalar_prefetch=1,
            grid=(1,),
            in_specs=[
                whole(slab, rows, width),
                whole(slab, rows, width),
                whole(2, slab, width),
                whole(2, slab, width),
                whole(2, slab, outs),
                whole(rows, width, outs),
            ],
            out_specs=whole(rows, width, outs),
        ),
        compiler_params=params(),
        cost_estimate=pl.CostEstimate(
            flops=2 * rows * width * 2 * slab * outs,
            bytes_accessed=8 * slab * rows * width + 6 * rows * width * outs,
            transcendentals=rows * width,
        ),
    )(pos, mixed, other, gain, bias, weights, gate)


def shards(
    pair,
    ln_gain,
    ln_bias,
    w_a_gate,
    w_a_proj,
    w_b_gate,
    w_b_proj,
    w_gate,
    out_gain,
    out_bias,
    w_out,
):
    rows, tokens, _ = pair.shape
    x_count, cores = lax.axis_size("x"), lax.axis_size("core")
    pos = jnp.stack([lax.axis_index("x"), lax.axis_index("core")]).astype(jnp.int32)
    width = tokens // x_count
    own_width = width // cores
    slab = w_a_gate.shape[1]

    weights = jnp.stack([w.T for w in (w_a_gate, w_a_proj, w_b_gate, w_b_proj)])
    weights = lax.all_gather(weights, "x", axis=1, tiled=True)
    half = x_count * slab
    left_weights = weights[:2].reshape(2 * half, -1)
    right_weights = weights[2:].reshape(2 * half, -1)

    normed = norm_columns(pos, pair, ln_gain, ln_bias, width)
    left = lax.all_to_all(project(normed, left_weights), "row", split_axis=0, concat_axis=0, tiled=True)
    left = lax.all_gather(left.reshape(tokens, width), "x")
    right = lax.all_to_all(project(normed, right_weights), "row", split_axis=0, concat_axis=0, tiled=True)
    right = right.reshape(tokens, width)
    gate = output_gate(pos, normed, w_gate, own_width)

    mixed = mix(pos, left, right, rows)
    mixed = lax.all_to_all(mixed, "row", split_axis=0, concat_axis=0, tiled=True)
    other = lax.ppermute(mixed[:, rows:], "core", [(0, 1), (1, 0)])

    def by_core(array):
        array = array.reshape(x_count, cores, slab, -1)
        return jnp.swapaxes(array, 0, 1).reshape(cores, half, -1)

    gain = jnp.broadcast_to(by_core(out_gain), (cores, half, own_width))
    bias = jnp.broadcast_to(by_core(out_bias), (cores, half, own_width))
    return finish(pos, mixed, other, gain, bias, by_core(w_out), gate)


def solution(mesh):
    cores = 2
    names = ("row", "x", "core")
    fine = Mesh(mesh.devices.reshape(mesh.devices.shape[0], -1, cores), names)
    chan = ("x", "core")
    in_specs = (
        P("row", None, None),
        P(),
        P(),
        P(None, chan),
        P(None, chan),
        P(None, chan),
        P(None, chan),
        P(),
        P(),
        P(),
        P(),
    )
    return jax.shard_map(shards, mesh=fine, in_specs=in_specs, out_specs=P("row", chan, None), check_vma=False)
```

```python
import jax
import jax.numpy as jnp
from jax import lax
from jax.experimental import pallas as pl
from jax.experimental.pallas import tpu as pltpu
from jax.sharding import Mesh
from jax.sharding import PartitionSpec as P

F32 = jnp.float32
BF16 = jnp.bfloat16
VMEM_LIMIT = 32 * 1024 * 1024
LARGE_LIMIT = 57 * 1024 * 1024
EPS = 1e-05
LANES = 128
SIDE = (0, 1, 1, 0)
NEXT = ((0, 1), (1, 0), (2, 3), (3, 2))
PAIRS = ((0, 3), (1, 2))
SWAP = ((0, 1), (1, 0))


def params(limit=VMEM_LIMIT):
    return pltpu.CompilerParams(vmem_limit_bytes=limit)


def whole(*shape):
    return pl.BlockSpec(shape, lambda s, pos: (0,) * len(shape))


def norm_kernel(pos, pair, gain, bias, out, held, sems):
    rows = pair.shape[0] // 2
    copies = []
    for part in range(4):
        row, side = part // 2 * rows, part % 2
        at = pl.multiple_of(pos[side] * LANES, LANES)
        copies.append(
            pltpu.make_async_copy(pair.at[pl.ds(row, rows), pl.ds(at, LANES), :], held.at[part], sems.at[part])
        )
    for copy in copies:
        copy.start()
    for part, copy in enumerate(copies):
        copy.wait()
        row, side = part // 2 * rows, part % 2
        values = held[part].astype(F32)
        mean = jnp.mean(values, axis=-1, keepdims=True)
        centred = values - mean
        var = jnp.mean(centred * centred, axis=-1, keepdims=True)
        normed = centred * lax.rsqrt(var + EPS) * gain[...] + bias[...]
        out[row : row + rows, side * LANES : (side + 1) * LANES, :] = normed.astype(BF16)


def norm_columns(pos, pair, gain, bias):
    rows, _, chans = pair.shape
    return pl.pallas_call(
        norm_kernel,
        out_shape=jax.ShapeDtypeStruct((rows, 2 * LANES, chans), BF16),
        grid_spec=pltpu.PrefetchScalarGridSpec(
            num_scalar_prefetch=1,
            grid=(1,),
            in_specs=[pl.BlockSpec(memory_space=pltpu.HBM), whole(1, 1, chans), whole(1, 1, chans)],
            out_specs=whole(rows, 2 * LANES, chans),
            scratch_shapes=[pltpu.VMEM((4, rows // 2, LANES, chans), BF16), pltpu.SemaphoreType.DMA((4,))],
        ),
        compiler_params=params(LARGE_LIMIT),
        cost_estimate=pl.CostEstimate(
            flops=16 * rows * LANES * chans, bytes_accessed=8 * rows * LANES * chans, transcendentals=2 * rows * LANES
        ),
    )(pos, pair, gain.reshape(1, 1, chans), bias.reshape(1, 1, chans))


def project_kernel(pos, normed, own, core, near, far, out, held):
    for place, part in enumerate((own, core, near, far)):
        held[0, pos[4 + place]] = part[0]
        held[1, pos[4 + place]] = part[1]
    rows, width, chans = normed.shape
    slab = held.shape[1] * held.shape[2]
    flat = normed[...].reshape(rows * width, chans)
    weights = held[...].reshape(2 * slab, chans)
    both = lax.dot_general(weights, flat, (((1,), (1,)), ((), ())), preferred_element_type=F32)
    value = jax.nn.sigmoid(both[:slab]) * both[slab:]
    parts = [value[:, k * width : (k + 1) * width] for k in range(rows)]
    out[...] = jnp.swapaxes(jnp.stack(parts, axis=0), 0, 1).astype(BF16)


def project(pos, normed, weights, which):
    rows, width, chans = normed.shape
    small = weights[0].shape[1]
    slab = 4 * small
    part = pl.BlockSpec((2, small, chans), lambda s, pos: (which, 0, 0))
    return pl.pallas_call(
        project_kernel,
        out_shape=jax.ShapeDtypeStruct((slab, rows, width), BF16),
        grid_spec=pltpu.PrefetchScalarGridSpec(
            num_scalar_prefetch=1,
            grid=(width // LANES,),
            in_specs=[pl.BlockSpec((rows, LANES, chans), lambda s, pos: (0, s, 0)), part, part, part, part],
            out_specs=pl.BlockSpec((slab, rows, LANES), lambda s, pos: (0, 0, s)),
            scratch_shapes=[pltpu.VMEM((2, 4, small, chans), BF16)],
        ),
        compiler_params=params(),
        cost_estimate=pl.CostEstimate(
            flops=4 * rows * width * slab * chans,
            bytes_accessed=2 * rows * width * (slab + chans),
            transcendentals=rows * width * slab,
        ),
    )(pos, normed, *weights)


def gate_kernel(pos, normed, weights, out):
    rows, width, chans = normed.shape
    flat = normed[...].reshape(rows * width, chans)
    got = jnp.dot(flat, weights[...], preferred_element_type=F32)
    out[...] = jax.nn.sigmoid(got).reshape(rows, width, chans)


def output_gate(pos, normed, weights):
    rows, _, chans = normed.shape
    step = rows // 2
    return pl.pallas_call(
        gate_kernel,
        out_shape=jax.ShapeDtypeStruct((rows, LANES, chans), F32),
        grid_spec=pltpu.PrefetchScalarGridSpec(
            num_scalar_prefetch=1,
            grid=(2,),
            in_specs=[pl.BlockSpec((step, LANES, chans), lambda s, pos: (s, pos[2], 0)), whole(chans, chans)],
            out_specs=pl.BlockSpec((step, LANES, chans), lambda s, pos: (s, 0, 0)),
        ),
        compiler_params=params(),
        cost_estimate=pl.CostEstimate(
            flops=2 * rows * LANES * chans * chans,
            bytes_accessed=6 * rows * LANES * chans,
            transcendentals=rows * LANES * chans,
        ),
    )(pos, normed, weights)


def mix_kernel(pos, right, own, core, near, far, out):
    per = LANES // out.shape[2]
    for place, left in enumerate((own, core, near, far)):
        mixed = lax.dot_general(left[...], right[...], (((0,), (0,)), ((), ())), preferred_element_type=F32)
        mixed = mixed.astype(BF16)
        for side in range(2):
            at = pos[8 + 2 * place + side] * per
            for half in range(2):
                block = mixed[side * LANES : (side + 1) * LANES, half * LANES : (half + 1) * LANES]
                out[pl.ds(at, per), half] = block.reshape(per, out.shape[2], LANES)


def mix(pos, right, lefts, rows):
    depth, width = right.shape
    tokens = 4 * width
    return pl.pallas_call(
        mix_kernel,
        out_shape=jax.ShapeDtypeStruct((tokens // rows, 2, rows, LANES), BF16),
        grid_spec=pltpu.PrefetchScalarGridSpec(
            num_scalar_prefetch=1,
            grid=(1,),
            in_specs=[whole(depth, width)] * 5,
            out_specs=whole(tokens // rows, 2, rows, LANES),
        ),
        compiler_params=params(),
        cost_estimate=pl.CostEstimate(
            flops=2 * depth * tokens * width, bytes_accessed=2 * (5 * depth * width + tokens * width), transcendentals=0
        ),
    )(pos, right, *lefts)


def finish_kernel(mixed, gain, bias, weights, gate, out):
    chans, rows, _ = mixed.shape
    values = mixed[...].astype(F32)
    values = values - (jnp.sum(values, axis=0) / chans)[None]
    scale = lax.rsqrt(jnp.sum(values * values, axis=0) / chans + EPS)
    scaled = jnp.swapaxes(values * scale[None], 0, 1)
    scaled = (scaled * gain[...][None] + bias[...][None]).astype(BF16)
    for row in range(rows):
        proj = lax.dot_general(
            scaled[row], weights[...], (((0,), (0,)), ((), ())), preferred_element_type=F32
        )
        out[row] = (proj * gate[row]).astype(BF16)


def finish(mixed, gain, bias, weights, gate):
    chans, rows, width = mixed.shape
    return pl.pallas_call(
        finish_kernel,
        out_shape=jax.ShapeDtypeStruct((rows, width, weights.shape[1]), BF16),
        compiler_params=params(),
        cost_estimate=pl.CostEstimate(
            flops=2 * rows * width * chans * chans, bytes_accessed=8 * chans * rows * width, transcendentals=rows * width
        ),
    )(mixed, gain, bias, weights, gate)


def positions(x, core):
    a = x // 2
    b = jnp.where(a == 0, x, 3 - x)
    slot = 2 * (x % 2) + core
    blocks = []
    for other_b, other_core in ((b, core), (b, 1 - core), (1 - b, core), (1 - b, 1 - core)):
        blocks += [2 * other_b + other_core, 2 * (3 - other_b) + other_core]
    slots = [slot, 2 * (x % 2) + 1 - core, 2 * (1 - x % 2) + core, 2 * (1 - x % 2) + 1 - core]
    return jnp.stack([blocks[0], blocks[1], a, a] + slots + blocks).astype(jnp.int32)


def shards(
    pair,
    ln_gain,
    ln_bias,
    w_a_gate,
    w_a_proj,
    w_b_gate,
    w_b_proj,
    w_gate,
    out_gain,
    out_bias,
    w_out,
):
    rows, tokens, chans = pair.shape
    depth = lax.axis_size("row")
    pos = positions(lax.axis_index("x"), lax.axis_index("core"))

    own = jnp.stack([w.T for w in (w_a_gate, w_a_proj, w_b_gate, w_b_proj)])
    diagonal = [(2 * f + c, 2 * t + 1 - c) for f, t in NEXT for c in range(2)]
    weights = [
        own,
        lax.ppermute(own, "core", SWAP),
        lax.ppermute(own, "x", NEXT),
        lax.ppermute(own, ("x", "core"), diagonal),
    ]
    normed = norm_columns(pos, pair, ln_gain, ln_bias)

    def spread(operand):
        return lax.all_to_all(operand, "row", split_axis=0, concat_axis=0, tiled=True).reshape(tokens, -1)

    left = spread(project(pos, normed, weights, 0))
    right = project(pos, normed, weights, 1)
    left, right = lax.optimization_barrier((left, right))
    near = lax.ppermute(left, "x", NEXT)
    core = lax.ppermute(left, "core", SWAP)
    right = spread(right)
    near, normed, out_gain, out_bias, w_out, right = lax.optimization_barrier(
        (near, normed, out_gain, out_bias, w_out, right)
    )
    far = lax.ppermute(near, "core", SWAP)

    def in_order(array):
        return jnp.swapaxes(array.reshape(2, depth, -1), 0, 1).reshape(2 * depth, -1)

    gate = output_gate(pos, normed, w_gate)
    gain = jnp.broadcast_to(in_order(out_gain), (2 * depth, LANES))
    bias = jnp.broadcast_to(in_order(out_bias), (2 * depth, LANES))
    out_weights = in_order(w_out)
    right, gate, gain, bias, out_weights = lax.optimization_barrier((right, gate, gain, bias, out_weights))

    mixed = mix(pos, right, (left, core, near, far), rows).reshape(2 * depth, rows, LANES)
    groups = [[4 * row + x for row in range(depth) for x in pair_of] for pair_of in PAIRS]
    mixed = lax.all_to_all(
        mixed, ("row", "x"), split_axis=0, concat_axis=0, tiled=True, axis_index_groups=groups
    )

    return finish(mixed, gain, bias, out_weights, gate)


def solution(mesh):
    fine = Mesh(mesh.devices.reshape(mesh.devices.shape[0], -1, 2), ("row", "x", "core"))
    chan = ("x", "core")
    in_specs = (
        P("row", None, None),
        P(),
        P(),
        P(None, chan),
        P(None, chan),
        P(None, chan),
        P(None, chan),
        P(),
        P(),
        P(),
        P(),
    )
    return jax.shard_map(shards, mesh=fine, in_specs=in_specs, out_specs=P("row", chan, None), check_vma=False)
```

```python
import jax
import jax.numpy as jnp
from jax import lax
from jax.experimental import pallas as pl
from jax.experimental.pallas import tpu as pltpu
from jax.sharding import Mesh
from jax.sharding import PartitionSpec as P

F32 = jnp.float32
BF16 = jnp.bfloat16
VMEM_LIMIT = 32 * 1024 * 1024
LARGE_LIMIT = 50 * 1024 * 1024
EPS = 1e-05
LANES = 128
SWAP = ((0, 1), (1, 0))
OVER_FIRST = (((0,), (0,)), ((), ()))
OVER_LAST = (((1,), (1,)), ((), ()))


def params(limit=VMEM_LIMIT):
    return pltpu.CompilerParams(vmem_limit_bytes=limit)


def whole(*shape):
    return pl.BlockSpec(shape, lambda s, pos: (0,) * len(shape))


def normalise(values, gain, bias):
    chans = values.shape[-1]
    share = jnp.full((chans, chans), 1.0 / chans, BF16)
    mean = jnp.dot(values, share, preferred_element_type=F32)
    centred = values.astype(F32) - mean
    square = centred * centred
    high = square.astype(BF16)
    low = (square - high.astype(F32)).astype(BF16)
    var = jnp.dot(high, share, preferred_element_type=F32) + jnp.dot(low, share, preferred_element_type=F32)
    return (centred * lax.rsqrt(var + EPS) * gain + bias).astype(BF16)


def front_kernel(pos, pair, scale, mine, theirs, out, own, weights):
    step, core = pl.program_id(0), pos[1]
    weights[:, core] = mine[...]
    weights[:, 1 - core] = theirs[...]
    rows, width, chans = pair.shape
    slab = 2 * mine.shape[1]
    normed = normalise(pair[...].reshape(rows * width, chans), scale[0:1], scale[1:2])

    @pl.when(step == pos[0])
    def _():
        own[...] = normed.reshape(rows, width, chans)

    got = lax.dot_general(
        weights[...].reshape(4 * slab, chans), normed, OVER_LAST, preferred_element_type=F32
    )

    def gated(at):
        value = jax.nn.sigmoid(got[at : at + slab]) * got[at + slab : at + 2 * slab]
        parts = [value[:, k * width : (k + 1) * width] for k in range(rows)]
        return jnp.swapaxes(jnp.stack(parts, axis=0), 0, 1).astype(BF16)

    left, right = gated(0), gated(2 * slab)
    out[pl.ds(step // 2 * slab, slab), step % 2] = left
    out[:slab, 2 + step] = right
    out[slab:, 2 + step] = right


def front(pos, pair, scale, mine, theirs):
    rows, tokens, chans = pair.shape
    steps = tokens // (2 * LANES)
    slab = 2 * mine.shape[1]
    return pl.pallas_call(
        front_kernel,
        out_shape=(
            jax.ShapeDtypeStruct((2 * slab, 2 + steps, rows, LANES), BF16),
            jax.ShapeDtypeStruct((rows, LANES, chans), BF16),
        ),
        grid_spec=pltpu.PrefetchScalarGridSpec(
            num_scalar_prefetch=1,
            grid=(steps,),
            in_specs=[
                pl.BlockSpec((rows, LANES, chans), lambda s, pos: (0, 2 * s + pos[1], 0)),
                whole(2, chans),
                whole(*mine.shape),
                whole(*theirs.shape),
            ],
            out_specs=(whole(2 * slab, 2 + steps, rows, LANES), whole(rows, LANES, chans)),
            scratch_shapes=[pltpu.VMEM((4, 2) + mine.shape[1:], BF16)],
        ),
        compiler_params=params(LARGE_LIMIT),
        cost_estimate=pl.CostEstimate(
            flops=14 * steps * rows * LANES * chans * chans,
            bytes_accessed=4 * steps * rows * LANES * chans,
            transcendentals=steps * rows * LANES * chans,
        ),
    )(pos, pair, scale, mine, theirs)


def gate_kernel(normed, weights, out):
    rows, width, chans = normed.shape
    flat = normed[...].reshape(rows * width, chans)
    got = jnp.dot(flat, weights[...], preferred_element_type=F32)
    out[...] = jax.nn.sigmoid(got).reshape(rows, width, chans)


def output_gate(normed, weights):
    rows, width, chans = normed.shape
    return pl.pallas_call(
        gate_kernel,
        out_shape=jax.ShapeDtypeStruct((rows, width, chans), F32),
        compiler_params=params(),
        cost_estimate=pl.CostEstimate(
            flops=2 * rows * width * chans * chans,
            bytes_accessed=6 * rows * width * chans,
            transcendentals=rows * width * chans,
        ),
    )(normed, weights)


def mix_kernel(pos, got, other, out):
    core = pos[1]
    sources, parts, rows, _ = got.shape
    per = LANES // rows

    def block(ref, at):
        return ref[:, at].reshape(sources * rows, LANES)

    right = jnp.concatenate([block(got, at) for at in range(2, parts)], axis=1)
    for ref, first in ((got, core), (other, 1 - core)):
        left = jnp.concatenate([block(ref, 0), block(ref, 1)], axis=1)
        mixed = lax.dot_general(left, right, OVER_FIRST, preferred_element_type=F32).astype(BF16)
        for side in range(2):
            for at in range(parts - 2):
                piece = mixed[side * LANES : (side + 1) * LANES, at * LANES : (at + 1) * LANES]
                out[pl.ds((2 * side + first) * per, per), at] = piece.reshape(per, rows, LANES)


def mix(pos, got, other):
    sources, parts, rows, _ = got.shape
    depth = sources * rows
    return pl.pallas_call(
        mix_kernel,
        out_shape=jax.ShapeDtypeStruct((4 * LANES // rows, parts - 2, rows, LANES), BF16),
        grid_spec=pltpu.PrefetchScalarGridSpec(
            num_scalar_prefetch=1,
            grid=(1,),
            in_specs=[whole(*got.shape), whole(*other.shape)],
            out_specs=whole(4 * LANES // rows, parts - 2, rows, LANES),
        ),
        compiler_params=params(),
        cost_estimate=pl.CostEstimate(
            flops=8 * depth * LANES * (parts - 2) * LANES, bytes_accessed=2 * depth * LANES * 12, transcendentals=0
        ),
    )(pos, got, other)


def finish_kernel(mixed, gain, bias, weights, gate, out):
    chans, rows, _ = mixed.shape
    values = mixed[...].astype(F32)
    values = values - (jnp.sum(values, axis=0) / chans)[None]
    scale = lax.rsqrt(jnp.sum(values * values, axis=0) / chans + EPS)
    scaled = jnp.swapaxes(values * scale[None], 0, 1)
    scaled = (scaled * gain[...][None] + bias[...][None]).astype(BF16)
    for row in range(rows):
        proj = lax.dot_general(scaled[row], weights[...], OVER_FIRST, preferred_element_type=F32)
        out[row] = (proj * gate[row]).astype(BF16)


def finish(mixed, gain, bias, weights, gate):
    chans, rows, width = mixed.shape
    return pl.pallas_call(
        finish_kernel,
        out_shape=jax.ShapeDtypeStruct((rows, width, weights.shape[1]), BF16),
        compiler_params=params(),
        cost_estimate=pl.CostEstimate(
            flops=2 * rows * width * chans * chans, bytes_accessed=8 * chans * rows * width, transcendentals=rows * width
        ),
    )(mixed, gain, bias, weights, gate)


def shards(
    pair,
    ln_gain,
    ln_bias,
    w_a_gate,
    w_a_proj,
    w_b_gate,
    w_b_proj,
    w_gate,
    out_gain,
    out_bias,
    w_out,
):
    rows = pair.shape[0]
    depth, x_count = lax.axis_size("row"), lax.axis_size("x")
    half = depth // 2
    pos = jnp.stack([lax.axis_index("x"), lax.axis_index("core")]).astype(jnp.int32)

    mine = jnp.stack([w.T for w in (w_a_gate, w_a_proj, w_b_gate, w_b_proj)])
    theirs = lax.ppermute(mine, "core", SWAP)
    messages, normed = front(pos, pair, jnp.stack([ln_gain, ln_bias]), mine, theirs)
    shape = messages.shape
    got = lax.all_to_all(
        messages.reshape(shape[0], -1, LANES), "row", split_axis=0, concat_axis=0, tiled=True
    ).reshape(shape)
    got, normed, w_gate, out_gain, out_bias, w_out = lax.optimization_barrier(
        (got, normed, w_gate, out_gain, out_bias, w_out)
    )
    other = lax.ppermute(got[:, :2], "core", SWAP)

    def in_order(array):
        return jnp.swapaxes(array.reshape(x_count, half, -1), 0, 1).reshape(x_count * half, -1)

    gate = output_gate(normed, w_gate)
    gain = jnp.broadcast_to(in_order(out_gain), (x_count * half, LANES))
    bias = jnp.broadcast_to(in_order(out_bias), (x_count * half, LANES))
    out_weights = in_order(w_out)
    got, gate, gain, bias, out_weights = lax.optimization_barrier((got, gate, gain, bias, out_weights))

    mixed = mix(pos, got, other).reshape(half * x_count, rows, LANES)
    groups = [[x_count * (part * half + at) + x for at in range(half) for x in range(x_count)] for part in range(2)]
    mixed = lax.all_to_all(
        mixed, ("row", "x"), split_axis=0, concat_axis=0, tiled=True, axis_index_groups=groups
    )
    return finish(mixed, gain, bias, out_weights, gate)


def solution(mesh):
    fine = Mesh(mesh.devices.reshape(mesh.devices.shape[0], -1, 2), ("row", "x", "core"))
    chan = ("x", "core")
    in_specs = (
        P("row", None, None),
        P(),
        P(),
        P(None, chan),
        P(None, chan),
        P(None, chan),
        P(None, chan),
        P(),
        P(),
        P(),
        P(),
    )
    return jax.shard_map(shards, mesh=fine, in_specs=in_specs, out_specs=P("row", chan, None), check_vma=False)
```

```python
import jax
import jax.numpy as jnp
from jax import lax
from jax.experimental import pallas as pl
from jax.experimental.pallas import tpu as pltpu
from jax.sharding import Mesh
from jax.sharding import PartitionSpec as P

F32 = jnp.float32
BF16 = jnp.bfloat16
VMEM_LIMIT = 32 * 1024 * 1024
LARGE_LIMIT = 50 * 1024 * 1024
EPS = 1e-05
LANES = 128
SWAP = ((0, 1), (1, 0))
OVER_FIRST = (((0,), (0,)), ((), ()))


def params(limit=VMEM_LIMIT):
    return pltpu.CompilerParams(vmem_limit_bytes=limit)


def in_vmem(count):
    return [pl.BlockSpec(memory_space=pltpu.VMEM)] * count


def normalise(values, gain, bias):
    values = values.T.astype(F32)
    centred = values - jnp.mean(values, axis=0, keepdims=True)
    var = jnp.mean(centred * centred, axis=0, keepdims=True)
    return (centred * lax.rsqrt(var + EPS) * gain + bias).astype(BF16)


def front_kernel(pair, scale, mine, theirs, out, own, weights, held, sems):
    core, x = lax.axis_index("core"), lax.axis_index("x")
    steps, rows, _, chans = held.shape
    copies = []
    for step in range(steps):
        at = pl.multiple_of((2 * step + core) * LANES, LANES)
        copies.append(pltpu.make_async_copy(pair.at[:, pl.ds(at, LANES), :], held.at[step], sems.at[step]))
    for copy in copies:
        copy.start()
    weights[:, core] = mine[...]
    weights[:, 1 - core] = theirs[...]
    slab = 2 * mine.shape[1]
    both = weights[...].reshape(4 * slab, chans)
    columns = scale[...].T
    for step in range(steps):
        copies[step].wait()
        normed = normalise(held[step].reshape(rows * LANES, chans), columns[:, 0:1], columns[:, 1:2])

        @pl.when(step == x)
        def _():
            own[...] = normed

        got = jnp.dot(both, normed, preferred_element_type=F32)

        def gated(first):
            value = jax.nn.sigmoid(got[first : first + slab]) * got[first + slab : first + 2 * slab]
            parts = [value[:, k * LANES : (k + 1) * LANES] for k in range(rows)]
            return jnp.swapaxes(jnp.stack(parts, axis=0), 0, 1).astype(BF16)

        left, right = gated(0), gated(2 * slab)
        half = step // 2 * slab
        out[half : half + slab, step % 2] = left
        out[:slab, 2 + step] = right
        out[slab:, 2 + step] = right


def front(pair, scale, mine, theirs):
    rows, tokens, chans = pair.shape
    steps = tokens // (2 * LANES)
    slab = 2 * mine.shape[1]
    return pl.pallas_call(
        front_kernel,
        out_shape=(
            jax.ShapeDtypeStruct((2 * slab, 2 + steps, rows, LANES), BF16),
            jax.ShapeDtypeStruct((chans, rows * LANES), BF16),
        ),
        in_specs=[pl.BlockSpec(memory_space=pltpu.HBM)] + in_vmem(3),
        out_specs=tuple(in_vmem(2)),
        scratch_shapes=[
            pltpu.VMEM((4, 2) + mine.shape[1:], BF16),
            pltpu.VMEM((steps, rows, LANES, chans), BF16),
            pltpu.SemaphoreType.DMA((steps,)),
        ],
        compiler_params=params(LARGE_LIMIT),
        cost_estimate=pl.CostEstimate(
            flops=14 * steps * rows * LANES * chans * chans,
            bytes_accessed=4 * steps * rows * LANES * chans,
            transcendentals=steps * rows * LANES * chans,
        ),
    )(pair, scale, mine, theirs)


def gate_kernel(normed, weights, out):
    got = lax.dot_general(normed[...], weights[...], OVER_FIRST, preferred_element_type=F32)
    out[...] = jax.nn.sigmoid(got).reshape(out.shape)


def output_gate(normed, weights):
    chans, pairs = normed.shape
    rows = pairs // LANES
    return pl.pallas_call(
        gate_kernel,
        out_shape=jax.ShapeDtypeStruct((rows, LANES, chans), F32),
        in_specs=in_vmem(2),
        out_specs=in_vmem(1)[0],
        compiler_params=params(),
        cost_estimate=pl.CostEstimate(
            flops=2 * pairs * chans * chans, bytes_accessed=6 * pairs * chans, transcendentals=pairs * chans
        ),
    )(normed, weights)


def mix_kernel(got, other, out):
    core = lax.axis_index("core")
    sources, parts, rows, _ = got.shape
    per = LANES // rows

    def block(ref, at):
        return ref[:, at].reshape(sources * rows, LANES)

    right = jnp.concatenate([block(got, at) for at in range(2, parts)], axis=1)
    for ref, first in ((got, core), (other, 1 - core)):
        left = jnp.concatenate([block(ref, 0), block(ref, 1)], axis=1)
        mixed = lax.dot_general(left, right, OVER_FIRST, preferred_element_type=F32).astype(BF16)
        for side in range(2):
            for at in range(parts - 2):
                piece = mixed[side * LANES : (side + 1) * LANES, at * LANES : (at + 1) * LANES]
                out[at, pl.ds((2 * side + first) * per, per)] = piece.reshape(per, rows, LANES)


def mix(got, other):
    sources, parts, rows, _ = got.shape
    depth = sources * rows
    return pl.pallas_call(
        mix_kernel,
        out_shape=jax.ShapeDtypeStruct((parts - 2, 4 * LANES // rows, rows, LANES), BF16),
        in_specs=in_vmem(2),
        out_specs=in_vmem(1)[0],
        compiler_params=params(),
        cost_estimate=pl.CostEstimate(
            flops=8 * depth * LANES * (parts - 2) * LANES, bytes_accessed=2 * depth * LANES * 12, transcendentals=0
        ),
    )(got, other)


def finish_kernel(mixed, gain, bias, weights, gate, out, held, sems):
    chans, rows, width = mixed.shape
    values = mixed[...].astype(F32)
    values = values - (jnp.sum(values, axis=0) / chans)[None]
    scale = lax.rsqrt(jnp.sum(values * values, axis=0) / chans + EPS)
    scaled = jnp.swapaxes(values * scale[None], 0, 1)
    scaled = (scaled * gain[...][None] + bias[...][None]).astype(BF16)
    count = held.shape[0]
    step = rows // count
    copies = []
    for piece in range(count):
        at = piece * step
        wide = jnp.concatenate([scaled[at + row] for row in range(step)], axis=1)
        proj = lax.dot_general(wide, weights[...], OVER_FIRST, preferred_element_type=F32)
        held[piece] = (proj.reshape(step, width, -1) * gate[at : at + step]).astype(BF16)
        copies.append(pltpu.make_async_copy(held.at[piece], out.at[pl.ds(at, step)], sems.at[piece]))
        copies[-1].start()
    for copy in copies:
        copy.wait()


def finish(mixed, gain, bias, weights, gate):
    chans, rows, width = mixed.shape
    outs = weights.shape[1]
    return pl.pallas_call(
        finish_kernel,
        out_shape=jax.ShapeDtypeStruct((rows, width, outs), BF16),
        in_specs=in_vmem(5),
        out_specs=pl.BlockSpec(memory_space=pltpu.HBM),
        scratch_shapes=[pltpu.VMEM((2, rows // 2, width, outs), BF16), pltpu.SemaphoreType.DMA((2,))],
        compiler_params=params(),
        cost_estimate=pl.CostEstimate(
            flops=2 * rows * width * chans * chans, bytes_accessed=8 * chans * rows * width, transcendentals=rows * width
        ),
    )(mixed, gain, bias, weights, gate)


def shards(
    pair,
    ln_gain,
    ln_bias,
    w_a_gate,
    w_a_proj,
    w_b_gate,
    w_b_proj,
    w_gate,
    out_gain,
    out_bias,
    w_out,
):
    rows, _, chans = pair.shape
    depth, x_count = lax.axis_size("row"), lax.axis_size("x")
    half = depth // 2

    mine = jnp.stack([w.T for w in (w_a_gate, w_a_proj, w_b_gate, w_b_proj)])
    theirs = lax.ppermute(mine, "core", SWAP)
    messages, normed = front(pair, jnp.stack([ln_gain, ln_bias]), mine, theirs)
    shape = messages.shape
    got = lax.all_to_all(
        messages.reshape(shape[0], -1, LANES), "row", split_axis=0, concat_axis=0, tiled=True
    ).reshape(shape)
    got, normed, w_gate, out_gain, out_bias = lax.optimization_barrier((got, normed, w_gate, out_gain, out_bias))
    other = lax.ppermute(got[:, :2], "core", SWAP)
    gate = output_gate(normed, w_gate)
    gain = jnp.broadcast_to(out_gain[:, None], (chans, LANES))
    bias = jnp.broadcast_to(out_bias[:, None], (chans, LANES))
    got, gate, gain, bias = lax.optimization_barrier((got, gate, gain, bias))

    mixed = mix(got, other).reshape(x_count * half, rows, LANES)
    groups = [[x_count * (part * half + at) + x for x in range(x_count) for at in range(half)] for part in range(2)]
    mixed = lax.all_to_all(
        mixed, ("row", "x"), split_axis=0, concat_axis=0, tiled=True, axis_index_groups=groups
    )
    return finish(mixed, gain, bias, w_out, gate)


def solution(mesh):
    fine = Mesh(mesh.devices.reshape(mesh.devices.shape[0], -1, 2), ("row", "x", "core"))
    chan = ("x", "core")
    in_specs = (
        P("row", None, None),
        P(),
        P(),
        P(None, chan),
        P(None, chan),
        P(None, chan),
        P(None, chan),
        P(),
        P(),
        P(),
        P(),
    )
    return jax.shard_map(shards, mesh=fine, in_specs=in_specs, out_specs=P("row", chan, None), check_vma=False)
```

```python
import jax
import jax.numpy as jnp
from jax import lax
from jax.experimental import pallas as pl
from jax.experimental.pallas import tpu as pltpu
from jax.sharding import Mesh
from jax.sharding import PartitionSpec as P

F32 = jnp.float32
BF16 = jnp.bfloat16
VMEM_LIMIT = 32 * 1024 * 1024
LARGE_LIMIT = 50 * 1024 * 1024
EPS = 1e-05
LANES = 128
SWAP = ((0, 1), (1, 0))
OVER_FIRST = (((0,), (0,)), ((), ()))


def params(limit=VMEM_LIMIT):
    return pltpu.CompilerParams(vmem_limit_bytes=limit)


def in_vmem(count):
    return [pl.BlockSpec(memory_space=pltpu.VMEM)] * count


def normalise(values, gain, bias):
    values = values.T.astype(F32)
    centred = values - jnp.mean(values, axis=0, keepdims=True)
    var = jnp.mean(centred * centred, axis=0, keepdims=True)
    return (centred * lax.rsqrt(var + EPS) * gain + bias).astype(BF16)


def front_kernel(pair, scale, mine, theirs, out, own, weights, held, sems):
    core, x = lax.axis_index("core"), lax.axis_index("x")
    steps, rows, _, chans = held.shape
    copies = []
    for step in range(steps):
        at = pl.multiple_of((2 * step + core) * LANES, LANES)
        copies.append(pltpu.make_async_copy(pair.at[:, pl.ds(at, LANES), :], held.at[step], sems.at[step]))
    for copy in copies:
        copy.start()
    weights[:, core] = mine[...]
    weights[:, 1 - core] = theirs[...]
    slab = 2 * mine.shape[1]
    both = weights[...].reshape(4 * slab, chans)
    columns = scale[...].T
    for step in range(steps):
        copies[step].wait()
        normed = normalise(held[step].reshape(rows * LANES, chans), columns[:, 0:1], columns[:, 1:2])

        @pl.when(step == x)
        def _():
            own[...] = normed

        got = jnp.dot(both, normed, preferred_element_type=F32)

        def gated(first):
            value = jax.nn.sigmoid(got[first : first + slab]) * got[first + slab : first + 2 * slab]
            parts = [value[:, k * LANES : (k + 1) * LANES] for k in range(rows)]
            return jnp.swapaxes(jnp.stack(parts, axis=0), 0, 1).astype(BF16)

        out[:, step] = gated(0)
        out[:, steps + step] = gated(2 * slab)


def front(pair, scale, mine, theirs):
    rows, tokens, chans = pair.shape
    steps = tokens // (2 * LANES)
    slab = 2 * mine.shape[1]
    return pl.pallas_call(
        front_kernel,
        out_shape=(
            jax.ShapeDtypeStruct((slab, 2 * steps, rows, LANES), BF16),
            jax.ShapeDtypeStruct((chans, rows * LANES), BF16),
        ),
        in_specs=[pl.BlockSpec(memory_space=pltpu.HBM)] + in_vmem(3),
        out_specs=tuple(in_vmem(2)),
        scratch_shapes=[
            pltpu.VMEM((4, 2) + mine.shape[1:], BF16),
            pltpu.VMEM((steps, rows, LANES, chans), BF16),
            pltpu.SemaphoreType.DMA((steps,)),
        ],
        compiler_params=params(LARGE_LIMIT),
        cost_estimate=pl.CostEstimate(
            flops=14 * steps * rows * LANES * chans * chans,
            bytes_accessed=4 * steps * rows * LANES * chans,
            transcendentals=steps * rows * LANES * chans,
        ),
    )(pair, scale, mine, theirs)


def gate_kernel(normed, weights, out):
    got = lax.dot_general(normed[...], weights[...], OVER_FIRST, preferred_element_type=F32)
    out[...] = jax.nn.sigmoid(got).reshape(out.shape)


def output_gate(normed, weights):
    chans, pairs = normed.shape
    rows = pairs // LANES
    return pl.pallas_call(
        gate_kernel,
        out_shape=jax.ShapeDtypeStruct((rows, LANES, chans), F32),
        in_specs=in_vmem(2),
        out_specs=in_vmem(1)[0],
        compiler_params=params(),
        cost_estimate=pl.CostEstimate(
            flops=2 * pairs * chans * chans, bytes_accessed=6 * pairs * chans, transcendentals=pairs * chans
        ),
    )(normed, weights)


def mix_kernel(got, other, out):
    core = lax.axis_index("core")
    sources, parts, rows, _ = got.shape
    blocks = parts // 2
    per = LANES // rows

    def joined(ref, first):
        return jnp.concatenate(
            [ref[:, first + at].reshape(sources * rows, LANES) for at in range(blocks)], axis=1
        )

    right = joined(got, blocks)
    for ref, first in ((got, core), (other, 1 - core)):
        mixed = lax.dot_general(joined(ref, 0), right, OVER_FIRST, preferred_element_type=F32).astype(BF16)
        for side in range(blocks):
            for at in range(blocks):
                piece = mixed[side * LANES : (side + 1) * LANES, at * LANES : (at + 1) * LANES]
                out[at, pl.ds((2 * side + first) * per, per)] = piece.reshape(per, rows, LANES)


def mix(got, other):
    sources, parts, rows, _ = got.shape
    depth, width = sources * rows, parts // 2 * LANES
    return pl.pallas_call(
        mix_kernel,
        out_shape=jax.ShapeDtypeStruct((parts // 2, 2 * width // rows, rows, LANES), BF16),
        in_specs=in_vmem(2),
        out_specs=in_vmem(1)[0],
        compiler_params=params(),
        cost_estimate=pl.CostEstimate(
            flops=4 * depth * width * width, bytes_accessed=2 * (3 * depth * width + 2 * width * width), transcendentals=0
        ),
    )(got, other)


def finish_kernel(mixed, gain, bias, weights, gate, out, held, sems):
    groups, _, each, rows, width = mixed.shape
    chans = groups * each
    values = (mixed[:, 0].astype(F32) + mixed[:, 1].astype(F32)).reshape(chans, rows, width)
    values = values - (jnp.sum(values, axis=0) / chans)[None]
    scale = lax.rsqrt(jnp.sum(values * values, axis=0) / chans + EPS)
    scaled = jnp.swapaxes(values * scale[None], 0, 1)
    scaled = (scaled * gain[...][None] + bias[...][None]).astype(BF16)
    count = held.shape[0]
    step = rows // count
    copies = []
    for piece in range(count):
        at = piece * step
        wide = jnp.concatenate([scaled[at + row] for row in range(step)], axis=1)
        proj = lax.dot_general(wide, weights[...], OVER_FIRST, preferred_element_type=F32)
        held[piece] = (proj.reshape(step, width, -1) * gate[at : at + step]).astype(BF16)
        copies.append(pltpu.make_async_copy(held.at[piece], out.at[pl.ds(at, step)], sems.at[piece]))
        copies[-1].start()
    for copy in copies:
        copy.wait()


def finish(mixed, gain, bias, weights, gate):
    groups, _, each, rows, width = mixed.shape
    chans, outs = weights.shape
    return pl.pallas_call(
        finish_kernel,
        out_shape=jax.ShapeDtypeStruct((rows, width, outs), BF16),
        in_specs=in_vmem(5),
        out_specs=pl.BlockSpec(memory_space=pltpu.HBM),
        scratch_shapes=[pltpu.VMEM((4, rows // 4, width, outs), BF16), pltpu.SemaphoreType.DMA((4,))],
        compiler_params=params(),
        cost_estimate=pl.CostEstimate(
            flops=2 * rows * width * chans * chans, bytes_accessed=10 * chans * rows * width, transcendentals=rows * width
        ),
    )(mixed, gain, bias, weights, gate)


def shards(
    pair,
    ln_gain,
    ln_bias,
    w_a_gate,
    w_a_proj,
    w_b_gate,
    w_b_proj,
    w_gate,
    out_gain,
    out_bias,
    w_out,
):
    rows, _, chans = pair.shape
    depth, x_count = lax.axis_size("row"), lax.axis_size("x")
    half = depth // 2

    mine = jnp.stack([w.T for w in (w_a_gate, w_a_proj, w_b_gate, w_b_proj)])
    theirs = lax.ppermute(mine, "core", SWAP)
    messages, normed = front(pair, jnp.stack([ln_gain, ln_bias]), mine, theirs)
    shape = messages.shape
    halves = [[part * half + at for at in range(half)] for part in range(2)]
    got = lax.all_to_all(
        messages.reshape(half, -1, LANES), "row", split_axis=0, concat_axis=0, tiled=True, axis_index_groups=halves
    ).reshape(shape)
    got, normed, w_gate, out_gain, out_bias = lax.optimization_barrier((got, normed, w_gate, out_gain, out_bias))
    other = lax.ppermute(got[:, : shape[1] // 2], "core", SWAP)
    gate = output_gate(normed, w_gate)
    gain = jnp.broadcast_to(out_gain[:, None], (chans, LANES))
    bias = jnp.broadcast_to(out_bias[:, None], (chans, LANES))
    got, gate, gain, bias = lax.optimization_barrier((got, gate, gain, bias))

    mixed = mix(got, other).reshape(x_count * depth, rows, LANES)
    group = [x_count * row + x for x in range(x_count) for row in range(depth)]
    mixed = lax.all_to_all(
        mixed, ("row", "x"), split_axis=0, concat_axis=0, tiled=True, axis_index_groups=[group]
    )
    return finish(mixed.reshape(x_count, 2, half, rows, LANES), gain, bias, w_out, gate)


def solution(mesh):
    fine = Mesh(mesh.devices.reshape(mesh.devices.shape[0], -1, 2), ("row", "x", "core"))
    chan = ("x", "core")
    in_specs = (
        P("row", None, None),
        P(),
        P(),
        P(None, chan),
        P(None, chan),
        P(None, chan),
        P(None, chan),
        P(),
        P(),
        P(),
        P(),
    )
    return jax.shard_map(shards, mesh=fine, in_specs=in_specs, out_specs=P("row", chan, None), check_vma=False)
```

```python
import jax
import jax.numpy as jnp
from jax import lax
from jax.experimental import pallas as pl
from jax.experimental.pallas import tpu as pltpu
from jax.sharding import Mesh
from jax.sharding import PartitionSpec as P

F32 = jnp.float32
BF16 = jnp.bfloat16
VMEM_LIMIT = 32 * 1024 * 1024
LARGE_LIMIT = 50 * 1024 * 1024
EPS = 1e-05
LANES = 128
SWAP = ((0, 1), (1, 0))
OVER_FIRST = (((0,), (0,)), ((), ()))


def params(limit=VMEM_LIMIT):
    return pltpu.CompilerParams(vmem_limit_bytes=limit)


def in_vmem(count):
    return [pl.BlockSpec(memory_space=pltpu.VMEM)] * count


def normalise(values, gain, bias):
    values = values.T.astype(F32)
    centred = values - jnp.mean(values, axis=0, keepdims=True)
    var = jnp.mean(centred * centred, axis=0, keepdims=True)
    return (centred * lax.rsqrt(var + EPS) * gain + bias).astype(BF16)


def front_kernel(pair, scale, mine, theirs, out, own, weights, held, sems):
    core, x = lax.axis_index("core"), lax.axis_index("x")
    steps, rows, _, chans = held.shape
    copies = []
    for step in range(steps):
        at = pl.multiple_of((2 * step + core) * LANES, LANES)
        copies.append(pltpu.make_async_copy(pair.at[:, pl.ds(at, LANES), :], held.at[step], sems.at[step]))
    for copy in copies:
        copy.start()
    weights[:, core] = mine[...]
    weights[:, 1 - core] = theirs[...]
    slab = 2 * mine.shape[1]
    both = weights[...].reshape(4 * slab, chans)
    columns = scale[...].T
    for step in range(steps):
        copies[step].wait()
        normed = normalise(held[step].reshape(rows * LANES, chans), columns[:, 0:1], columns[:, 1:2])

        @pl.when(step == x)
        def _():
            own[...] = normed

        got = jnp.dot(both, normed, preferred_element_type=F32)

        def gated(first):
            value = jax.nn.sigmoid(got[first : first + slab]) * got[first + slab : first + 2 * slab]
            parts = [value[:, k * LANES : (k + 1) * LANES] for k in range(rows)]
            return jnp.swapaxes(jnp.stack(parts, axis=0), 0, 1).astype(BF16)

        out[:, step] = gated(0)
        out[:, steps + step] = gated(2 * slab)


def front(pair, scale, mine, theirs):
    rows, tokens, chans = pair.shape
    steps = tokens // (2 * LANES)
    slab = 2 * mine.shape[1]
    return pl.pallas_call(
        front_kernel,
        out_shape=(
            jax.ShapeDtypeStruct((slab, 2 * steps, rows, LANES), BF16),
            jax.ShapeDtypeStruct((chans, rows * LANES), BF16),
        ),
        in_specs=[pl.BlockSpec(memory_space=pltpu.HBM)] + in_vmem(3),
        out_specs=tuple(in_vmem(2)),
        scratch_shapes=[
            pltpu.VMEM((4, 2) + mine.shape[1:], BF16),
            pltpu.VMEM((steps, rows, LANES, chans), BF16),
            pltpu.SemaphoreType.DMA((steps,)),
        ],
        compiler_params=params(LARGE_LIMIT),
        cost_estimate=pl.CostEstimate(
            flops=14 * steps * rows * LANES * chans * chans,
            bytes_accessed=4 * steps * rows * LANES * chans,
            transcendentals=steps * rows * LANES * chans,
        ),
    )(pair, scale, mine, theirs)


def gate_kernel(normed, weights, out):
    got = lax.dot_general(normed[...], weights[...], OVER_FIRST, preferred_element_type=F32)
    out[...] = jax.nn.sigmoid(got).reshape(out.shape)


def output_gate(normed, weights):
    chans, pairs = normed.shape
    rows = pairs // LANES
    return pl.pallas_call(
        gate_kernel,
        out_shape=jax.ShapeDtypeStruct((rows, LANES, chans), F32),
        in_specs=in_vmem(2),
        out_specs=in_vmem(1)[0],
        compiler_params=params(),
        cost_estimate=pl.CostEstimate(
            flops=2 * pairs * chans * chans, bytes_accessed=6 * pairs * chans, transcendentals=pairs * chans
        ),
    )(normed, weights)


def mix_kernel(got, other, out):
    core = lax.axis_index("core")
    sources, parts, rows, _ = got.shape
    blocks = parts // 2
    per = LANES // rows

    def joined(ref, first):
        return jnp.concatenate(
            [ref[:, first + at].reshape(sources * rows, LANES) for at in range(blocks)], axis=1
        )

    right = joined(got, blocks)
    for ref, first in ((got, core), (other, 1 - core)):
        mixed = lax.dot_general(joined(ref, 0), right, OVER_FIRST, preferred_element_type=F32).astype(BF16)
        for side in range(blocks):
            for at in range(blocks):
                piece = mixed[side * LANES : (side + 1) * LANES, at * LANES : (at + 1) * LANES]
                out[:, 2 * side + first, at] = piece.reshape(per, rows, LANES)


def mix(got, other):
    sources, parts, rows, _ = got.shape
    depth, width = sources * rows, parts // 2 * LANES
    return pl.pallas_call(
        mix_kernel,
        out_shape=jax.ShapeDtypeStruct((LANES // rows, parts, parts // 2, rows, LANES), BF16),
        in_specs=in_vmem(2),
        out_specs=in_vmem(1)[0],
        compiler_params=params(),
        cost_estimate=pl.CostEstimate(
            flops=4 * depth * width * width, bytes_accessed=2 * (3 * depth * width + 2 * width * width), transcendentals=0
        ),
    )(got, other)


def finish_kernel(mixed, gain, bias, weights, gate, out, held, sems):
    groups, _, each, rows, width = mixed.shape
    chans = groups * each
    values = (mixed[:, 0].astype(F32) + mixed[:, 1].astype(F32)).reshape(chans, rows, width)
    values = values - (jnp.sum(values, axis=0) / chans)[None]
    scale = lax.rsqrt(jnp.sum(values * values, axis=0) / chans + EPS)
    scaled = jnp.swapaxes(values * scale[None], 0, 1)
    scaled = (scaled * gain[...][None] + bias[...][None]).astype(BF16)
    count = held.shape[0]
    step = rows // count
    copies = []
    for piece in range(count):
        at = piece * step
        wide = jnp.concatenate([scaled[at + row] for row in range(step)], axis=1)
        proj = lax.dot_general(wide, weights[...], OVER_FIRST, preferred_element_type=F32)
        held[piece] = (proj.reshape(step, width, -1) * gate[at : at + step]).astype(BF16)
        copies.append(pltpu.make_async_copy(held.at[piece], out.at[pl.ds(at, step)], sems.at[piece]))
        copies[-1].start()
    for copy in copies:
        copy.wait()


def finish(mixed, gain, bias, weights, gate):
    groups, _, each, rows, width = mixed.shape
    chans, outs = weights.shape
    return pl.pallas_call(
        finish_kernel,
        out_shape=jax.ShapeDtypeStruct((rows, width, outs), BF16),
        in_specs=in_vmem(5),
        out_specs=pl.BlockSpec(memory_space=pltpu.HBM),
        scratch_shapes=[pltpu.VMEM((4, rows // 4, width, outs), BF16), pltpu.SemaphoreType.DMA((4,))],
        compiler_params=params(),
        cost_estimate=pl.CostEstimate(
            flops=2 * rows * width * chans * chans, bytes_accessed=10 * chans * rows * width, transcendentals=rows * width
        ),
    )(mixed, gain, bias, weights, gate)


def shards(
    pair,
    ln_gain,
    ln_bias,
    w_a_gate,
    w_a_proj,
    w_b_gate,
    w_b_proj,
    w_gate,
    out_gain,
    out_bias,
    w_out,
):
    rows, _, chans = pair.shape
    depth, x_count = lax.axis_size("row"), lax.axis_size("x")
    half = depth // 2

    mine = jnp.stack([w.T for w in (w_a_gate, w_a_proj, w_b_gate, w_b_proj)])
    theirs = lax.ppermute(mine, "core", SWAP)
    messages, normed = front(pair, jnp.stack([ln_gain, ln_bias]), mine, theirs)
    shape = messages.shape
    per = LANES // rows
    z_count = depth // per
    halves = [
        [z * per + y for y in range(per) for z in range(part * z_count // 2, (part + 1) * z_count // 2)]
        for part in range(2)
    ]
    got = lax.all_to_all(
        messages.reshape(half, -1, LANES), "row", split_axis=0, concat_axis=0, tiled=True, axis_index_groups=halves
    ).reshape(shape)
    got, normed, w_gate, out_gain, out_bias, w_out = lax.optimization_barrier(
        (got, normed, w_gate, out_gain, out_bias, w_out)
    )
    other = lax.ppermute(got[:, : shape[1] // 2], "core", SWAP)
    gate = output_gate(normed, w_gate)

    def in_order(array):
        return jnp.swapaxes(array.reshape(x_count, half, -1), 0, 1).reshape(chans, -1)

    gain = jnp.broadcast_to(in_order(out_gain), (chans, LANES))
    bias = jnp.broadcast_to(in_order(out_bias), (chans, LANES))
    got, gate, gain, bias, out_weights = lax.optimization_barrier((got, gate, gain, bias, in_order(w_out)))

    mixed = mix(got, other).reshape(depth * x_count, rows, LANES)
    group = [x_count * (z * per + y) + x for y in range(per) for z in range(z_count) for x in range(x_count)]
    mixed = lax.all_to_all(
        mixed, ("row", "x"), split_axis=0, concat_axis=0, tiled=True, axis_index_groups=[group]
    )
    mixed = mixed.reshape(per, 2, z_count // 2 * x_count, rows, LANES)
    return finish(mixed, gain, bias, out_weights, gate)


def solution(mesh):
    fine = Mesh(mesh.devices.reshape(mesh.devices.shape[0], -1, 2), ("row", "x", "core"))
    chan = ("x", "core")
    in_specs = (
        P("row", None, None),
        P(),
        P(),
        P(None, chan),
        P(None, chan),
        P(None, chan),
        P(None, chan),
        P(),
        P(),
        P(),
        P(),
    )
    return jax.shard_map(shards, mesh=fine, in_specs=in_specs, out_specs=P("row", chan, None), check_vma=False)
```

```python
import jax
import jax.numpy as jnp
from jax import lax
from jax.experimental import pallas as pl
from jax.experimental.pallas import tpu as pltpu
from jax.sharding import Mesh
from jax.sharding import PartitionSpec as P

F32 = jnp.float32
BF16 = jnp.bfloat16
VMEM_LIMIT = 32 * 1024 * 1024
LARGE_LIMIT = 50 * 1024 * 1024
EPS = 1e-05
LANES = 128
SWAP = ((0, 1), (1, 0))
OVER_FIRST = (((0,), (0,)), ((), ()))


def params(limit=VMEM_LIMIT):
    return pltpu.CompilerParams(vmem_limit_bytes=limit)


def in_vmem(count):
    return [pl.BlockSpec(memory_space=pltpu.VMEM)] * count


def measure_kernel(pair, values, stats, held, sems):
    core = lax.axis_index("core")
    steps, rows, _, chans = held.shape
    copies = []
    for step in range(steps):
        at = pl.multiple_of((2 * step + core) * LANES, LANES)
        copies.append(pltpu.make_async_copy(pair.at[:, pl.ds(at, LANES), :], held.at[step], sems.at[step]))
    for copy in copies:
        copy.start()
    for step in range(steps):
        copies[step].wait()
        block = held[step].reshape(rows * LANES, chans).T
        values[step] = block
        block = block.astype(F32)
        mean = jnp.mean(block, axis=0, keepdims=True)
        centred = block - mean
        var = jnp.mean(centred * centred, axis=0, keepdims=True)
        stats[step, 0:1] = mean
        stats[step, 1:2] = lax.rsqrt(var + EPS)


def measure_columns(pair):
    rows, tokens, chans = pair.shape
    steps = tokens // (2 * LANES)
    return pl.pallas_call(
        measure_kernel,
        out_shape=(
            jax.ShapeDtypeStruct((steps, chans, rows * LANES), BF16),
            jax.ShapeDtypeStruct((steps, 2, rows * LANES), F32),
        ),
        in_specs=[pl.BlockSpec(memory_space=pltpu.HBM)],
        out_specs=tuple(in_vmem(2)),
        scratch_shapes=[pltpu.VMEM((steps, rows, LANES, chans), BF16), pltpu.SemaphoreType.DMA((steps,))],
        compiler_params=params(LARGE_LIMIT),
        cost_estimate=pl.CostEstimate(
            flops=6 * steps * rows * LANES * chans,
            bytes_accessed=4 * steps * rows * LANES * chans,
            transcendentals=steps * rows * LANES,
        ),
    )(pair)


def project_kernel(values, stats, gain, bias, mine, theirs, out, own, weights):
    core, x = lax.axis_index("core"), lax.axis_index("x")
    weights[:, core] = mine[...]
    weights[:, 1 - core] = theirs[...]
    steps, chans, pairs = values.shape
    slab = 2 * mine.shape[1]
    both = weights[...].reshape(4 * slab, chans)
    gains, biases = gain[...].T, bias[...].T
    for step in range(steps):
        normed = (values[step].astype(F32) - stats[step, 0:1]) * stats[step, 1:2]
        normed = (normed * gains + biases).astype(BF16)

        @pl.when(step == x)
        def _():
            own[...] = normed

        got = jnp.dot(both, normed, preferred_element_type=F32)

        def gated(first):
            value = jax.nn.sigmoid(got[first : first + slab]) * got[first + slab : first + 2 * slab]
            parts = [value[:, at : at + LANES] for at in range(0, pairs, LANES)]
            return jnp.swapaxes(jnp.stack(parts, axis=0), 0, 1).astype(BF16)

        out[:, step] = gated(0)
        out[:, steps + step] = gated(2 * slab)


def project(values, stats, gain, bias, mine, theirs):
    steps, chans, pairs = values.shape
    slab = 2 * mine.shape[1]
    return pl.pallas_call(
        project_kernel,
        out_shape=(
            jax.ShapeDtypeStruct((slab, 2 * steps, pairs // LANES, LANES), BF16),
            jax.ShapeDtypeStruct((chans, pairs), BF16),
        ),
        in_specs=in_vmem(6),
        out_specs=tuple(in_vmem(2)),
        scratch_shapes=[pltpu.VMEM((4, 2) + mine.shape[1:], BF16)],
        compiler_params=params(),
        cost_estimate=pl.CostEstimate(
            flops=8 * steps * pairs * slab * chans,
            bytes_accessed=4 * steps * pairs * chans,
            transcendentals=2 * steps * pairs * slab,
        ),
    )(values, stats, gain.reshape(1, chans), bias.reshape(1, chans), mine, theirs)


def gate_kernel(normed, weights, out):
    got = lax.dot_general(normed[...], weights[...], OVER_FIRST, preferred_element_type=F32)
    out[...] = jax.nn.sigmoid(got).reshape(out.shape)


def output_gate(normed, weights):
    chans, pairs = normed.shape
    rows = pairs // LANES
    return pl.pallas_call(
        gate_kernel,
        out_shape=jax.ShapeDtypeStruct((rows, LANES, chans), F32),
        in_specs=in_vmem(2),
        out_specs=in_vmem(1)[0],
        compiler_params=params(),
        cost_estimate=pl.CostEstimate(
            flops=2 * pairs * chans * chans, bytes_accessed=6 * pairs * chans, transcendentals=pairs * chans
        ),
    )(normed, weights)


def mix_rows(got, left, first, out):
    sources, parts, rows, _ = got.shape
    blocks = parts // 2

    def joined(ref, start):
        return jnp.concatenate(
            [ref[:, start + at].reshape(sources * rows, LANES) for at in range(blocks)], axis=1
        )

    mixed = lax.dot_general(joined(left, 0), joined(got, blocks), OVER_FIRST, preferred_element_type=F32)
    mixed = mixed.astype(BF16)
    for side in range(blocks):
        for at in range(blocks):
            piece = mixed[side * LANES : (side + 1) * LANES, at * LANES : (at + 1) * LANES]
            out[:, 2 * side + first, at] = piece.reshape(LANES // rows, rows, LANES)


def mix_own_kernel(got, out):
    mix_rows(got, got, 0, out)


def mix_other_kernel(got, other, begun, out):
    core = lax.axis_index("core")
    for side in range(got.shape[1] // 2):
        out[:, 2 * side + core] = begun[:, 2 * side]
    mix_rows(got, other, 1 - core, out)


def mix(got, other):
    sources, parts, rows, _ = got.shape
    depth, width = sources * rows, parts // 2 * LANES
    shape = jax.ShapeDtypeStruct((LANES // rows, parts, parts // 2, rows, LANES), BF16)
    cost = pl.CostEstimate(
        flops=2 * depth * width * width, bytes_accessed=2 * (2 * depth * width + width * width), transcendentals=0
    )
    begun = pl.pallas_call(
        mix_own_kernel,
        out_shape=shape,
        in_specs=in_vmem(1),
        out_specs=in_vmem(1)[0],
        compiler_params=params(),
        cost_estimate=cost,
    )(got)
    return pl.pallas_call(
        mix_other_kernel,
        out_shape=shape,
        in_specs=in_vmem(3),
        out_specs=in_vmem(1)[0],
        compiler_params=params(),
        cost_estimate=cost,
    )(got, other, begun)


def finish_kernel(mixed, gain, bias, weights, gate, out, held, sems):
    groups, _, each, rows, width = mixed.shape
    chans = groups * each
    values = (mixed[:, 0].astype(F32) + mixed[:, 1].astype(F32)).reshape(chans, rows, width)
    values = values - (jnp.sum(values, axis=0) / chans)[None]
    scale = lax.rsqrt(jnp.sum(values * values, axis=0) / chans + EPS)
    scaled = jnp.swapaxes(values * scale[None], 0, 1)
    scaled = (scaled * gain[...][None] + bias[...][None]).astype(BF16)
    count = held.shape[0]
    step = rows // count
    copies = []
    for piece in range(count):
        at = piece * step
        wide = jnp.concatenate([scaled[at + row] for row in range(step)], axis=1)
        proj = lax.dot_general(wide, weights[...], OVER_FIRST, preferred_element_type=F32)
        held[piece] = (proj.reshape(step, width, -1) * gate[at : at + step]).astype(BF16)
        copies.append(pltpu.make_async_copy(held.at[piece], out.at[pl.ds(at, step)], sems.at[piece]))
        copies[-1].start()
    for copy in copies:
        copy.wait()


def finish(mixed, gain, bias, weights, gate):
    groups, _, each, rows, width = mixed.shape
    chans, outs = weights.shape
    return pl.pallas_call(
        finish_kernel,
        out_shape=jax.ShapeDtypeStruct((rows, width, outs), BF16),
        in_specs=in_vmem(5),
        out_specs=pl.BlockSpec(memory_space=pltpu.HBM),
        scratch_shapes=[pltpu.VMEM((4, rows // 4, width, outs), BF16), pltpu.SemaphoreType.DMA((4,))],
        compiler_params=params(),
        cost_estimate=pl.CostEstimate(
            flops=2 * rows * width * chans * chans, bytes_accessed=10 * chans * rows * width, transcendentals=rows * width
        ),
    )(mixed, gain, bias, weights, gate)


def shards(
    pair,
    ln_gain,
    ln_bias,
    w_a_gate,
    w_a_proj,
    w_b_gate,
    w_b_proj,
    w_gate,
    out_gain,
    out_bias,
    w_out,
):
    rows, _, chans = pair.shape
    depth, x_count = lax.axis_size("row"), lax.axis_size("x")
    half = depth // 2

    mine = jnp.stack([w.T for w in (w_a_gate, w_a_proj, w_b_gate, w_b_proj)])
    theirs = lax.ppermute(mine, "core", SWAP)
    values, stats = measure_columns(pair)
    messages, normed = project(values, stats, ln_gain, ln_bias, mine, theirs)
    shape = messages.shape
    per = LANES // rows
    z_count = depth // per
    halves = [
        [z * per + y for y in range(per) for z in range(part * z_count // 2, (part + 1) * z_count // 2)]
        for part in range(2)
    ]
    got = lax.all_to_all(
        messages.reshape(half, -1, LANES), "row", split_axis=0, concat_axis=0, tiled=True, axis_index_groups=halves
    ).reshape(shape)
    got, normed, w_gate, out_gain, out_bias, w_out = lax.optimization_barrier(
        (got, normed, w_gate, out_gain, out_bias, w_out)
    )
    other = lax.ppermute(got[:, : shape[1] // 2], "core", SWAP)
    gate = output_gate(normed, w_gate)

    def in_order(array):
        return jnp.swapaxes(array.reshape(x_count, half, -1), 0, 1).reshape(chans, -1)

    gain = jnp.broadcast_to(in_order(out_gain), (chans, LANES))
    bias = jnp.broadcast_to(in_order(out_bias), (chans, LANES))
    got, gate, gain, bias, out_weights = lax.optimization_barrier((got, gate, gain, bias, in_order(w_out)))

    mixed = mix(got, other).reshape(depth * x_count, rows, LANES)
    group = [x_count * (z * per + y) + x for y in range(per) for z in range(z_count) for x in range(x_count)]
    mixed = lax.all_to_all(
        mixed, ("row", "x"), split_axis=0, concat_axis=0, tiled=True, axis_index_groups=[group]
    )
    mixed = mixed.reshape(per, 2, z_count // 2 * x_count, rows, LANES)
    return finish(mixed, gain, bias, out_weights, gate)


def solution(mesh):
    fine = Mesh(mesh.devices.reshape(mesh.devices.shape[0], -1, 2), ("row", "x", "core"))
    chan = ("x", "core")
    in_specs = (
        P("row", None, None),
        P(),
        P(),
        P(None, chan),
        P(None, chan),
        P(None, chan),
        P(None, chan),
        P(),
        P(),
        P(),
        P(),
    )
    return jax.shard_map(shards, mesh=fine, in_specs=in_specs, out_specs=P("row", chan, None), check_vma=False)
```

```python
import jax
import jax.numpy as jnp
from jax import lax
from jax.experimental import pallas as pl
from jax.experimental.pallas import tpu as pltpu
from jax.sharding import Mesh
from jax.sharding import PartitionSpec as P

F32 = jnp.float32
BF16 = jnp.bfloat16
VMEM_LIMIT = 32 * 1024 * 1024
LARGE_LIMIT = 50 * 1024 * 1024
EPS = 1e-05
LANES = 128
SWAP = ((0, 1), (1, 0))
OVER_FIRST = (((0,), (0,)), ((), ()))


def params(limit=VMEM_LIMIT):
    return pltpu.CompilerParams(vmem_limit_bytes=limit)


def in_vmem(count):
    return [pl.BlockSpec(memory_space=pltpu.VMEM)] * count


def measure_kernel(pair, values, stats, held, sems):
    core = lax.axis_index("core")
    steps, rows, _, chans = held.shape
    copies = []
    for step in range(steps):
        at = pl.multiple_of((2 * step + core) * LANES, LANES)
        copies.append(pltpu.make_async_copy(pair.at[:, pl.ds(at, LANES), :], held.at[step], sems.at[step]))
    for copy in copies:
        copy.start()
    for step in range(steps):
        copies[step].wait()
        block = held[step].reshape(rows * LANES, chans).T
        values[step] = block
        block = block.astype(F32)
        mean = jnp.mean(block, axis=0, keepdims=True)
        centred = block - mean
        var = jnp.mean(centred * centred, axis=0, keepdims=True)
        stats[step, 0:1] = mean
        stats[step, 1:2] = lax.rsqrt(var + EPS)


def measure_columns(pair):
    rows, tokens, chans = pair.shape
    steps = tokens // (2 * LANES)
    return pl.pallas_call(
        measure_kernel,
        out_shape=(
            jax.ShapeDtypeStruct((steps, chans, rows * LANES), BF16),
            jax.ShapeDtypeStruct((steps, 2, rows * LANES), F32),
        ),
        in_specs=[pl.BlockSpec(memory_space=pltpu.HBM)],
        out_specs=tuple(in_vmem(2)),
        scratch_shapes=[pltpu.VMEM((steps, rows, LANES, chans), BF16), pltpu.SemaphoreType.DMA((steps,))],
        compiler_params=params(LARGE_LIMIT),
        cost_estimate=pl.CostEstimate(
            flops=6 * steps * rows * LANES * chans,
            bytes_accessed=4 * steps * rows * LANES * chans,
            transcendentals=steps * rows * LANES,
        ),
    )(pair)


def project_kernel(values, stats, gain, bias, mine, theirs, out, normed_out, weights):
    core = lax.axis_index("core")
    weights[:, core] = mine[...]
    weights[:, 1 - core] = theirs[...]
    steps, chans, pairs = values.shape
    slab = 2 * mine.shape[1]
    both = weights[...].reshape(4 * slab, chans)
    gains, biases = gain[...].T, bias[...].T
    for step in range(steps):
        normed = (values[step].astype(F32) - stats[step, 0:1]) * stats[step, 1:2]
        normed = (normed * gains + biases).astype(BF16)
        normed_out[step] = normed
        got = jnp.dot(both, normed, preferred_element_type=F32)

        def gated(first):
            value = jax.nn.sigmoid(got[first : first + slab]) * got[first + slab : first + 2 * slab]
            parts = [value[:, at : at + LANES] for at in range(0, pairs, LANES)]
            return jnp.swapaxes(jnp.stack(parts, axis=0), 0, 1).astype(BF16)

        out[:, step] = gated(0)
        out[:, steps + step] = gated(2 * slab)


def project(values, stats, gain, bias, mine, theirs):
    steps, chans, pairs = values.shape
    slab = 2 * mine.shape[1]
    return pl.pallas_call(
        project_kernel,
        out_shape=(
            jax.ShapeDtypeStruct((slab, 2 * steps, pairs // LANES, LANES), BF16),
            jax.ShapeDtypeStruct((steps, chans, pairs), BF16),
        ),
        in_specs=in_vmem(6),
        out_specs=tuple(in_vmem(2)),
        scratch_shapes=[pltpu.VMEM((4, 2) + mine.shape[1:], BF16)],
        compiler_params=params(),
        cost_estimate=pl.CostEstimate(
            flops=8 * steps * pairs * slab * chans,
            bytes_accessed=4 * steps * pairs * chans,
            transcendentals=2 * steps * pairs * slab,
        ),
    )(values, stats, gain.reshape(1, chans), bias.reshape(1, chans), mine, theirs)


def gate_kernel(normed, weights, out):
    got = lax.dot_general(normed[lax.axis_index("x")], weights[...], OVER_FIRST, preferred_element_type=F32)
    out[...] = jax.nn.sigmoid(got).reshape(out.shape)


def output_gate(normed, weights):
    _, chans, pairs = normed.shape
    rows = pairs // LANES
    return pl.pallas_call(
        gate_kernel,
        out_shape=jax.ShapeDtypeStruct((rows, LANES, chans), F32),
        in_specs=in_vmem(2),
        out_specs=in_vmem(1)[0],
        compiler_params=params(),
        cost_estimate=pl.CostEstimate(
            flops=2 * pairs * chans * chans, bytes_accessed=6 * pairs * chans, transcendentals=pairs * chans
        ),
    )(normed, weights)


def mix_rows(got, left, first, out):
    sources, parts, rows, _ = got.shape
    blocks = parts // 2

    def joined(ref, start):
        return jnp.concatenate(
            [ref[:, start + at].reshape(sources * rows, LANES) for at in range(blocks)], axis=1
        )

    mixed = lax.dot_general(joined(left, 0), joined(got, blocks), OVER_FIRST, preferred_element_type=F32)
    mixed = mixed.astype(BF16)
    for side in range(blocks):
        for at in range(blocks):
            piece = mixed[side * LANES : (side + 1) * LANES, at * LANES : (at + 1) * LANES]
            out[:, 2 * side + first, at] = piece.reshape(LANES // rows, rows, LANES)


def mix_own_kernel(got, out):
    mix_rows(got, got, 0, out)


def mix_other_kernel(got, other, begun, out):
    core = lax.axis_index("core")
    for side in range(got.shape[1] // 2):
        out[:, 2 * side + core] = begun[:, 2 * side]
    mix_rows(got, other, 1 - core, out)


def mix(got, other):
    sources, parts, rows, _ = got.shape
    depth, width = sources * rows, parts // 2 * LANES
    shape = jax.ShapeDtypeStruct((LANES // rows, parts, parts // 2, rows, LANES), BF16)
    cost = pl.CostEstimate(
        flops=2 * depth * width * width, bytes_accessed=2 * (2 * depth * width + width * width), transcendentals=0
    )
    begun = pl.pallas_call(
        mix_own_kernel,
        out_shape=shape,
        in_specs=in_vmem(1),
        out_specs=in_vmem(1)[0],
        compiler_params=params(),
        cost_estimate=cost,
    )(got)
    return pl.pallas_call(
        mix_other_kernel,
        out_shape=shape,
        in_specs=in_vmem(3),
        out_specs=in_vmem(1)[0],
        compiler_params=params(),
        cost_estimate=cost,
    )(got, other, begun)


def finish_kernel(mixed, gain, bias, weights, gate, out, held, sems):
    groups, _, each, rows, width = mixed.shape
    chans = groups * each
    values = (mixed[:, 0].astype(F32) + mixed[:, 1].astype(F32)).reshape(chans, rows, width)
    values = values - (jnp.sum(values, axis=0) / chans)[None]
    scale = lax.rsqrt(jnp.sum(values * values, axis=0) / chans + EPS)
    scaled = jnp.swapaxes(values * scale[None], 0, 1)
    scaled = (scaled * gain[...][None] + bias[...][None]).astype(BF16)
    count = held.shape[0]
    step = rows // count
    copies = []
    for piece in range(count):
        at = piece * step
        wide = jnp.concatenate([scaled[at + row] for row in range(step)], axis=1)
        proj = lax.dot_general(wide, weights[...], OVER_FIRST, preferred_element_type=F32)
        held[piece] = (proj.reshape(step, width, -1) * gate[at : at + step]).astype(BF16)
        copies.append(pltpu.make_async_copy(held.at[piece], out.at[pl.ds(at, step)], sems.at[piece]))
        copies[-1].start()
    for copy in copies:
        copy.wait()


def finish(mixed, gain, bias, weights, gate):
    groups, _, each, rows, width = mixed.shape
    chans, outs = weights.shape
    return pl.pallas_call(
        finish_kernel,
        out_shape=jax.ShapeDtypeStruct((rows, width, outs), BF16),
        in_specs=in_vmem(5),
        out_specs=pl.BlockSpec(memory_space=pltpu.HBM),
        scratch_shapes=[pltpu.VMEM((2, rows // 2, width, outs), BF16), pltpu.SemaphoreType.DMA((2,))],
        compiler_params=params(),
        cost_estimate=pl.CostEstimate(
            flops=2 * rows * width * chans * chans, bytes_accessed=10 * chans * rows * width, transcendentals=rows * width
        ),
    )(mixed, gain, bias, weights, gate)


def shards(
    pair,
    ln_gain,
    ln_bias,
    w_a_gate,
    w_a_proj,
    w_b_gate,
    w_b_proj,
    w_gate,
    out_gain,
    out_bias,
    w_out,
):
    rows, _, chans = pair.shape
    depth, x_count = lax.axis_size("row"), lax.axis_size("x")
    half = depth // 2

    mine = jnp.stack([w.T for w in (w_a_gate, w_a_proj, w_b_gate, w_b_proj)])
    theirs = lax.ppermute(mine, "core", SWAP)
    values, stats = measure_columns(pair)
    messages, normed = project(values, stats, ln_gain, ln_bias, mine, theirs)
    shape = messages.shape
    per = LANES // rows
    z_count = depth // per
    halves = [
        [z * per + y for y in range(per) for z in range(part * z_count // 2, (part + 1) * z_count // 2)]
        for part in range(2)
    ]
    got = lax.all_to_all(
        messages.reshape(half, -1, LANES), "row", split_axis=0, concat_axis=0, tiled=True, axis_index_groups=halves
    ).reshape(shape)
    got, normed, w_gate, out_gain, out_bias, w_out = lax.optimization_barrier(
        (got, normed, w_gate, out_gain, out_bias, w_out)
    )
    other = lax.ppermute(got[:, : shape[1] // 2], "core", SWAP)
    gate = output_gate(normed, w_gate)

    def in_order(array):
        return jnp.swapaxes(array.reshape(x_count, half, -1), 0, 1).reshape(chans, -1)

    gain = jnp.broadcast_to(in_order(out_gain), (chans, LANES))
    bias = jnp.broadcast_to(in_order(out_bias), (chans, LANES))
    got, gate, gain, bias, out_weights = lax.optimization_barrier((got, gate, gain, bias, in_order(w_out)))

    mixed = mix(got, other).reshape(depth * x_count, rows, LANES)
    group = [x_count * (z * per + y) + x for y in range(per) for z in range(z_count) for x in range(x_count)]
    mixed = lax.all_to_all(
        mixed, ("row", "x"), split_axis=0, concat_axis=0, tiled=True, axis_index_groups=[group]
    )
    mixed = mixed.reshape(per, 2, z_count // 2 * x_count, rows, LANES)
    return finish(mixed, gain, bias, out_weights, gate)


def solution(mesh):
    fine = Mesh(mesh.devices.reshape(mesh.devices.shape[0], -1, 2), ("row", "x", "core"))
    chan = ("x", "core")
    in_specs = (
        P("row", None, None),
        P(),
        P(),
        P(None, chan),
        P(None, chan),
        P(None, chan),
        P(None, chan),
        P(),
        P(),
        P(),
        P(),
    )
    return jax.shard_map(shards, mesh=fine, in_specs=in_specs, out_specs=P("row", chan, None), check_vma=False)
```

```python
import jax
import jax.numpy as jnp
from jax import lax
from jax.experimental import pallas as pl
from jax.experimental.pallas import tpu as pltpu
from jax.sharding import Mesh
from jax.sharding import PartitionSpec as P

F32 = jnp.float32
BF16 = jnp.bfloat16
VMEM_LIMIT = 32 * 1024 * 1024
LARGE_LIMIT = 50 * 1024 * 1024
EPS = 1e-05
LANES = 128
SWAP = ((0, 1), (1, 0))
OVER_FIRST = (((0,), (0,)), ((), ()))


def params(limit=VMEM_LIMIT):
    return pltpu.CompilerParams(vmem_limit_bytes=limit)


def in_vmem(count):
    return [pl.BlockSpec(memory_space=pltpu.VMEM)] * count


def measure_kernel(pair, values, stats, held, sems):
    core = lax.axis_index("core")
    steps, rows, _, chans = held.shape
    copies = []
    for step in range(steps):
        at = pl.multiple_of((2 * step + core) * LANES, LANES)
        copies.append(pltpu.make_async_copy(pair.at[:, pl.ds(at, LANES), :], held.at[step], sems.at[step]))
    for copy in copies:
        copy.start()
    for step in range(steps):
        copies[step].wait()
        block = held[step].reshape(rows * LANES, chans).T
        values[step] = block
        block = block.astype(F32)
        mean = jnp.mean(block, axis=0, keepdims=True)
        centred = block - mean
        var = jnp.mean(centred * centred, axis=0, keepdims=True)
        stats[step, 0:1] = mean
        stats[step, 1:2] = lax.rsqrt(var + EPS)


def measure_columns(pair):
    rows, tokens, chans = pair.shape
    steps = tokens // (2 * LANES)
    return pl.pallas_call(
        measure_kernel,
        out_shape=(
            jax.ShapeDtypeStruct((steps, chans, rows * LANES), BF16),
            jax.ShapeDtypeStruct((steps, 2, rows * LANES), F32),
        ),
        in_specs=[pl.BlockSpec(memory_space=pltpu.HBM)],
        out_specs=tuple(in_vmem(2)),
        scratch_shapes=[pltpu.VMEM((steps, rows, LANES, chans), BF16), pltpu.SemaphoreType.DMA((steps,))],
        compiler_params=params(LARGE_LIMIT),
        cost_estimate=pl.CostEstimate(
            flops=6 * steps * rows * LANES * chans,
            bytes_accessed=4 * steps * rows * LANES * chans,
            transcendentals=steps * rows * LANES,
        ),
    )(pair)


def project_kernel(values, stats, gain, bias, mine, theirs, out, own, weights, held):
    core, x = lax.axis_index("core"), lax.axis_index("x")
    weights[:, core] = mine[...]
    weights[:, 1 - core] = theirs[...]
    steps, chans, pairs = values.shape
    slab = 2 * mine.shape[1]
    both = weights[...].reshape(4 * slab, chans)
    gains, biases = gain[...].T, bias[...].T
    for step in range(steps):
        normed = (values[step].astype(F32) - stats[step, 0:1]) * stats[step, 1:2]
        normed = (normed * gains + biases).astype(BF16)
        held[step] = normed
        got = jnp.dot(both, normed, preferred_element_type=F32)

        def gated(first):
            value = jax.nn.sigmoid(got[first : first + slab]) * got[first + slab : first + 2 * slab]
            parts = [value[:, at : at + LANES] for at in range(0, pairs, LANES)]
            return jnp.swapaxes(jnp.stack(parts, axis=0), 0, 1).astype(BF16)

        out[:, step] = gated(0)
        out[:, steps + step] = gated(2 * slab)
    own[...] = held[x]


def project(values, stats, gain, bias, mine, theirs):
    steps, chans, pairs = values.shape
    slab = 2 * mine.shape[1]
    return pl.pallas_call(
        project_kernel,
        out_shape=(
            jax.ShapeDtypeStruct((slab, 2 * steps, pairs // LANES, LANES), BF16),
            jax.ShapeDtypeStruct((chans, pairs), BF16),
        ),
        in_specs=in_vmem(6),
        out_specs=tuple(in_vmem(2)),
        scratch_shapes=[pltpu.VMEM((4, 2) + mine.shape[1:], BF16), pltpu.VMEM(values.shape, BF16)],
        compiler_params=params(),
        cost_estimate=pl.CostEstimate(
            flops=8 * steps * pairs * slab * chans,
            bytes_accessed=4 * steps * pairs * chans,
            transcendentals=2 * steps * pairs * slab,
        ),
    )(values, stats, gain.reshape(1, chans), bias.reshape(1, chans), mine, theirs)


def gate_kernel(normed, weights, out):
    got = lax.dot_general(normed[...], weights[...], OVER_FIRST, preferred_element_type=F32)
    out[...] = jax.nn.sigmoid(got).reshape(out.shape)


def output_gate(normed, weights):
    chans, pairs = normed.shape
    rows = pairs // LANES
    return pl.pallas_call(
        gate_kernel,
        out_shape=jax.ShapeDtypeStruct((rows, LANES, chans), F32),
        in_specs=in_vmem(2),
        out_specs=in_vmem(1)[0],
        compiler_params=params(),
        cost_estimate=pl.CostEstimate(
            flops=2 * pairs * chans * chans, bytes_accessed=6 * pairs * chans, transcendentals=pairs * chans
        ),
    )(normed, weights)


def mix_rows(got, left, first, out):
    sources, parts, rows, _ = got.shape
    blocks = parts // 2

    def joined(ref, start):
        return jnp.concatenate(
            [ref[:, start + at].reshape(sources * rows, LANES) for at in range(blocks)], axis=1
        )

    mixed = lax.dot_general(joined(left, 0), joined(got, blocks), OVER_FIRST, preferred_element_type=F32)
    mixed = mixed.astype(BF16)
    for side in range(blocks):
        for at in range(blocks):
            piece = mixed[side * LANES : (side + 1) * LANES, at * LANES : (at + 1) * LANES]
            out[:, 2 * side + first, at] = piece.reshape(LANES // rows, rows, LANES)


def mix_own_kernel(got, out):
    mix_rows(got, got, 0, out)


def mix_other_kernel(got, other, begun, out):
    core = lax.axis_index("core")
    for side in range(got.shape[1] // 2):
        out[:, 2 * side + core] = begun[:, 2 * side]
    mix_rows(got, other, 1 - core, out)


def mix(got, other):
    sources, parts, rows, _ = got.shape
    depth, width = sources * rows, parts // 2 * LANES
    shape = jax.ShapeDtypeStruct((LANES // rows, parts, parts // 2, rows, LANES), BF16)
    cost = pl.CostEstimate(
        flops=2 * depth * width * width, bytes_accessed=2 * (2 * depth * width + width * width), transcendentals=0
    )
    begun = pl.pallas_call(
        mix_own_kernel,
        out_shape=shape,
        in_specs=in_vmem(1),
        out_specs=in_vmem(1)[0],
        compiler_params=params(),
        cost_estimate=cost,
    )(got)
    return pl.pallas_call(
        mix_other_kernel,
        out_shape=shape,
        in_specs=in_vmem(3),
        out_specs=in_vmem(1)[0],
        compiler_params=params(),
        cost_estimate=cost,
    )(got, other, begun)


def finish_kernel(mixed, gain, bias, weights, gate, out, held, sems):
    groups, _, each, rows, width = mixed.shape
    chans = groups * each
    values = (mixed[:, 0].astype(F32) + mixed[:, 1].astype(F32)).reshape(chans, rows, width)
    values = values - (jnp.sum(values, axis=0) / chans)[None]
    scale = lax.rsqrt(jnp.sum(values * values, axis=0) / chans + EPS)
    scaled = jnp.swapaxes(values * scale[None], 0, 1)
    scaled = (scaled * gain[...][None] + bias[...][None]).astype(BF16)
    count = held.shape[0]
    step = rows // count
    copies = []
    for piece in range(count):
        at = piece * step
        wide = jnp.concatenate([scaled[at + row] for row in range(step)], axis=1)
        proj = lax.dot_general(wide, weights[...], OVER_FIRST, preferred_element_type=F32)
        held[piece] = (proj.reshape(step, width, -1) * gate[at : at + step]).astype(BF16)
        copies.append(pltpu.make_async_copy(held.at[piece], out.at[pl.ds(at, step)], sems.at[piece]))
        copies[-1].start()
    for copy in copies:
        copy.wait()


def finish(mixed, gain, bias, weights, gate):
    groups, _, each, rows, width = mixed.shape
    chans, outs = weights.shape
    return pl.pallas_call(
        finish_kernel,
        out_shape=jax.ShapeDtypeStruct((rows, width, outs), BF16),
        in_specs=in_vmem(5),
        out_specs=pl.BlockSpec(memory_space=pltpu.HBM),
        scratch_shapes=[pltpu.VMEM((2, rows // 2, width, outs), BF16), pltpu.SemaphoreType.DMA((2,))],
        compiler_params=params(),
        cost_estimate=pl.CostEstimate(
            flops=2 * rows * width * chans * chans, bytes_accessed=10 * chans * rows * width, transcendentals=rows * width
        ),
    )(mixed, gain, bias, weights, gate)


def shards(
    pair,
    ln_gain,
    ln_bias,
    w_a_gate,
    w_a_proj,
    w_b_gate,
    w_b_proj,
    w_gate,
    out_gain,
    out_bias,
    w_out,
):
    rows, _, chans = pair.shape
    depth, x_count = lax.axis_size("row"), lax.axis_size("x")
    half = depth // 2

    mine = jnp.stack([w.T for w in (w_a_gate, w_a_proj, w_b_gate, w_b_proj)])
    theirs = lax.ppermute(mine, "core", SWAP)
    values, stats = measure_columns(pair)
    messages, normed = project(values, stats, ln_gain, ln_bias, mine, theirs)
    shape = messages.shape
    per = LANES // rows
    z_count = depth // per
    halves = [
        [z * per + y for y in range(per) for z in range(part * z_count // 2, (part + 1) * z_count // 2)]
        for part in range(2)
    ]
    got = lax.all_to_all(
        messages.reshape(half, -1, LANES), "row", split_axis=0, concat_axis=0, tiled=True, axis_index_groups=halves
    ).reshape(shape)
    got, normed, w_gate, out_gain, out_bias, w_out = lax.optimization_barrier(
        (got, normed, w_gate, out_gain, out_bias, w_out)
    )
    other = lax.ppermute(got[:, : shape[1] // 2], "core", SWAP)
    gate = output_gate(normed, w_gate)

    def in_order(array):
        return jnp.swapaxes(array.reshape(x_count, half, -1), 0, 1).reshape(chans, -1)

    gain = jnp.broadcast_to(in_order(out_gain), (chans, LANES))
    bias = jnp.broadcast_to(in_order(out_bias), (chans, LANES))
    got, gate, gain, bias, out_weights = lax.optimization_barrier((got, gate, gain, bias, in_order(w_out)))

    mixed = mix(got, other).reshape(depth * x_count, rows, LANES)
    group = [x_count * (z * per + y) + x for y in range(per) for z in range(z_count) for x in range(x_count)]
    mixed = lax.all_to_all(
        mixed, ("row", "x"), split_axis=0, concat_axis=0, tiled=True, axis_index_groups=[group]
    )
    mixed = mixed.reshape(per, 2, z_count // 2 * x_count, rows, LANES)
    return finish(mixed, gain, bias, out_weights, gate)


def solution(mesh):
    fine = Mesh(mesh.devices.reshape(mesh.devices.shape[0], -1, 2), ("row", "x", "core"))
    chan = ("x", "core")
    in_specs = (
        P("row", None, None),
        P(),
        P(),
        P(None, chan),
        P(None, chan),
        P(None, chan),
        P(None, chan),
        P(),
        P(),
        P(),
        P(),
    )
    return jax.shard_map(shards, mesh=fine, in_specs=in_specs, out_specs=P("row", chan, None), check_vma=False)
```

```python
import jax
import jax.numpy as jnp
from jax import lax
from jax.experimental import pallas as pl
from jax.experimental.pallas import tpu as pltpu
from jax.sharding import Mesh
from jax.sharding import PartitionSpec as P

F32 = jnp.float32
BF16 = jnp.bfloat16
VMEM_LIMIT = 32 * 1024 * 1024
LARGE_LIMIT = 50 * 1024 * 1024
EPS = 1e-05
LANES = 128
SWAP = ((0, 1), (1, 0))
OVER_FIRST = (((0,), (0,)), ((), ()))


def params(limit=VMEM_LIMIT):
    return pltpu.CompilerParams(vmem_limit_bytes=limit)


def in_vmem(count):
    return [pl.BlockSpec(memory_space=pltpu.VMEM)] * count


def measure_kernel(pair, values, stats, held, sems):
    core = lax.axis_index("core")
    steps, rows, _, chans = held.shape
    copies = []
    for step in range(steps):
        at = pl.multiple_of((2 * step + core) * LANES, LANES)
        copies.append(pltpu.make_async_copy(pair.at[:, pl.ds(at, LANES), :], held.at[step], sems.at[step]))
    for copy in copies:
        copy.start()
    for step in range(steps):
        copies[step].wait()
        block = held[step].reshape(rows * LANES, chans).T
        values[step] = block
        block = block.astype(F32)
        mean = jnp.mean(block, axis=0, keepdims=True)
        centred = block - mean
        var = jnp.mean(centred * centred, axis=0, keepdims=True)
        stats[step, 0:1] = mean
        stats[step, 1:2] = lax.rsqrt(var + EPS)


def measure_columns(pair):
    rows, tokens, chans = pair.shape
    steps = tokens // (2 * LANES)
    return pl.pallas_call(
        measure_kernel,
        out_shape=(
            jax.ShapeDtypeStruct((steps, chans, rows * LANES), BF16),
            jax.ShapeDtypeStruct((steps, 2, rows * LANES), F32),
        ),
        in_specs=[pl.BlockSpec(memory_space=pltpu.HBM)],
        out_specs=tuple(in_vmem(2)),
        scratch_shapes=[pltpu.VMEM((steps, rows, LANES, chans), BF16), pltpu.SemaphoreType.DMA((steps,))],
        compiler_params=params(LARGE_LIMIT),
        cost_estimate=pl.CostEstimate(
            flops=6 * steps * rows * LANES * chans,
            bytes_accessed=4 * steps * rows * LANES * chans,
            transcendentals=steps * rows * LANES,
        ),
    )(pair)


def project_kernel(values, stats, gain, bias, mine, theirs, out, own, weights, held):
    core, x = lax.axis_index("core"), lax.axis_index("x")
    weights[:, core] = mine[...]
    weights[:, 1 - core] = theirs[...]
    steps, chans, pairs = values.shape
    slab = 2 * mine.shape[1]
    both = weights[...].reshape(4 * slab, chans)
    gains, biases = gain[...].T, bias[...].T
    for step in range(steps):
        normed = (values[step].astype(F32) - stats[step, 0:1]) * stats[step, 1:2]
        normed = (normed * gains + biases).astype(BF16)
        held[step] = normed
        got = jnp.dot(both, normed, preferred_element_type=F32)

        def gated(first):
            value = jax.nn.sigmoid(got[first : first + slab]) * got[first + slab : first + 2 * slab]
            parts = [value[:, at : at + LANES] for at in range(0, pairs, LANES)]
            return jnp.swapaxes(jnp.stack(parts, axis=0), 0, 1).astype(BF16)

        out[:, step] = gated(0)
        out[:, steps + step] = gated(2 * slab)
    own[...] = held[x]


def project(values, stats, gain, bias, mine, theirs):
    steps, chans, pairs = values.shape
    slab = 2 * mine.shape[1]
    return pl.pallas_call(
        project_kernel,
        out_shape=(
            jax.ShapeDtypeStruct((slab, 2 * steps, pairs // LANES, LANES), BF16),
            jax.ShapeDtypeStruct((chans, pairs), BF16),
        ),
        in_specs=in_vmem(6),
        out_specs=tuple(in_vmem(2)),
        scratch_shapes=[pltpu.VMEM((4, 2) + mine.shape[1:], BF16), pltpu.VMEM(values.shape, BF16)],
        compiler_params=params(),
        cost_estimate=pl.CostEstimate(
            flops=8 * steps * pairs * slab * chans,
            bytes_accessed=4 * steps * pairs * chans,
            transcendentals=2 * steps * pairs * slab,
        ),
    )(values, stats, gain.reshape(1, chans), bias.reshape(1, chans), mine, theirs)


def gate_kernel(normed, weights, out):
    got = lax.dot_general(normed[...], weights[...], OVER_FIRST, preferred_element_type=F32)
    out[...] = jax.nn.sigmoid(got).reshape(out.shape)


def output_gate(normed, weights):
    chans, pairs = normed.shape
    rows = pairs // LANES
    return pl.pallas_call(
        gate_kernel,
        out_shape=jax.ShapeDtypeStruct((rows, LANES, chans), F32),
        in_specs=in_vmem(2),
        out_specs=in_vmem(1)[0],
        compiler_params=params(),
        cost_estimate=pl.CostEstimate(
            flops=2 * pairs * chans * chans, bytes_accessed=6 * pairs * chans, transcendentals=pairs * chans
        ),
    )(normed, weights)


def mix_rows(got, left, first, out):
    sources, parts, rows, _ = got.shape
    blocks = parts // 2

    def joined(ref, start):
        return jnp.concatenate(
            [ref[:, start + at].reshape(sources * rows, LANES) for at in range(blocks)], axis=1
        )

    mixed = lax.dot_general(joined(left, 0), joined(got, blocks), OVER_FIRST, preferred_element_type=F32)
    mixed = mixed.astype(BF16)
    for side in range(blocks):
        for at in range(blocks):
            piece = mixed[side * LANES : (side + 1) * LANES, at * LANES : (at + 1) * LANES]
            out[:, 2 * side + first, at] = piece.reshape(LANES // rows, rows, LANES)


def mix_own_kernel(got, out):
    mix_rows(got, got, 0, out)


def mix_other_kernel(got, other, begun, out):
    core = lax.axis_index("core")
    for side in range(got.shape[1] // 2):
        out[:, 2 * side + core] = begun[:, 2 * side]
    mix_rows(got, other, 1 - core, out)


def mix(got, other):
    sources, parts, rows, _ = got.shape
    depth, width = sources * rows, parts // 2 * LANES
    shape = jax.ShapeDtypeStruct((LANES // rows, parts, parts // 2, rows, LANES), BF16)
    cost = pl.CostEstimate(
        flops=2 * depth * width * width, bytes_accessed=2 * (2 * depth * width + width * width), transcendentals=0
    )
    begun = pl.pallas_call(
        mix_own_kernel,
        out_shape=shape,
        in_specs=in_vmem(1),
        out_specs=in_vmem(1)[0],
        compiler_params=params(),
        cost_estimate=cost,
    )(got)
    return pl.pallas_call(
        mix_other_kernel,
        out_shape=shape,
        in_specs=in_vmem(3),
        out_specs=in_vmem(1)[0],
        compiler_params=params(),
        cost_estimate=cost,
    )(got, other, begun)


def finish_kernel(mixed, gain, bias, weights, gate, out, held, sems):
    _, chans, rows, width = mixed.shape
    values = mixed[0].astype(F32) + mixed[1].astype(F32)
    values = values - (jnp.sum(values, axis=0) / chans)[None]
    scale = lax.rsqrt(jnp.sum(values * values, axis=0) / chans + EPS)
    scaled = jnp.swapaxes(values * scale[None], 0, 1)
    scaled = (scaled * gain[...][None] + bias[...][None]).astype(BF16)
    count = held.shape[0]
    step = rows // count
    copies = []
    for piece in range(count):
        at = piece * step
        wide = jnp.concatenate([scaled[at + row] for row in range(step)], axis=1)
        proj = lax.dot_general(wide, weights[...], OVER_FIRST, preferred_element_type=F32)
        held[piece] = (proj.reshape(step, width, -1) * gate[at : at + step]).astype(BF16)
        copies.append(pltpu.make_async_copy(held.at[piece], out.at[pl.ds(at, step)], sems.at[piece]))
        copies[-1].start()
    for copy in copies:
        copy.wait()


def finish(mixed, gain, bias, weights, gate):
    _, _, rows, width = mixed.shape
    chans, outs = weights.shape
    return pl.pallas_call(
        finish_kernel,
        out_shape=jax.ShapeDtypeStruct((rows, width, outs), BF16),
        in_specs=in_vmem(5),
        out_specs=pl.BlockSpec(memory_space=pltpu.HBM),
        scratch_shapes=[pltpu.VMEM((2, rows // 2, width, outs), BF16), pltpu.SemaphoreType.DMA((2,))],
        compiler_params=params(),
        cost_estimate=pl.CostEstimate(
            flops=2 * rows * width * chans * chans, bytes_accessed=10 * chans * rows * width, transcendentals=rows * width
        ),
    )(mixed, gain, bias, weights, gate)


def shards(
    pair,
    ln_gain,
    ln_bias,
    w_a_gate,
    w_a_proj,
    w_b_gate,
    w_b_proj,
    w_gate,
    out_gain,
    out_bias,
    w_out,
):
    rows, _, chans = pair.shape
    depth, x_count = lax.axis_size("row"), lax.axis_size("x")
    half = depth // 2

    mine = jnp.stack([w.T for w in (w_a_gate, w_a_proj, w_b_gate, w_b_proj)])
    theirs = lax.ppermute(mine, "core", SWAP)
    values, stats = measure_columns(pair)
    messages, normed = project(values, stats, ln_gain, ln_bias, mine, theirs)
    shape = messages.shape
    per = LANES // rows
    z_count = depth // per
    halves = [
        [z * per + y for z in range(z_count) for y in range(part * per // 2, (part + 1) * per // 2)] for part in range(2)
    ]
    got = lax.all_to_all(
        messages.reshape(half, -1, LANES), "row", split_axis=0, concat_axis=0, tiled=True, axis_index_groups=halves
    ).reshape(shape)
    got, normed, w_gate, out_gain, out_bias, w_out = lax.optimization_barrier(
        (got, normed, w_gate, out_gain, out_bias, w_out)
    )
    other = lax.ppermute(got[:, : shape[1] // 2], "core", SWAP)
    gate = output_gate(normed, w_gate)

    def in_order(array):
        array = array.reshape(x_count, z_count, per // 2, -1)
        return jnp.transpose(array, (2, 1, 0, 3)).reshape(chans, -1)

    gain = jnp.broadcast_to(in_order(out_gain), (chans, LANES))
    bias = jnp.broadcast_to(in_order(out_bias), (chans, LANES))
    got, gate, gain, bias, out_weights = lax.optimization_barrier((got, gate, gain, bias, in_order(w_out)))

    mixed = mix(got, other).reshape(depth * x_count, rows, LANES)
    group = [x_count * (z * per + y) + x for y in range(per) for z in range(z_count) for x in range(x_count)]
    mixed = lax.all_to_all(
        mixed, ("row", "x"), split_axis=0, concat_axis=0, tiled=True, axis_index_groups=[group]
    )
    mixed = mixed.reshape(2, chans, rows, LANES)
    return finish(mixed, gain, bias, out_weights, gate)


def solution(mesh):
    fine = Mesh(mesh.devices.reshape(mesh.devices.shape[0], -1, 2), ("row", "x", "core"))
    chan = ("x", "core")
    in_specs = (
        P("row", None, None),
        P(),
        P(),
        P(None, chan),
        P(None, chan),
        P(None, chan),
        P(None, chan),
        P(),
        P(),
        P(),
        P(),
    )
    return jax.shard_map(shards, mesh=fine, in_specs=in_specs, out_specs=P("row", chan, None), check_vma=False)
```

```python
import jax
import jax.numpy as jnp
from jax import lax
from jax.experimental import pallas as pl
from jax.experimental.pallas import tpu as pltpu
from jax.sharding import Mesh
from jax.sharding import PartitionSpec as P

F32 = jnp.float32
BF16 = jnp.bfloat16
VMEM_LIMIT = 32 * 1024 * 1024
LARGE_LIMIT = 50 * 1024 * 1024
EPS = 1e-05
LANES = 128
SWAP = ((0, 1), (1, 0))
OVER_FIRST = (((0,), (0,)), ((), ()))


def params(limit=VMEM_LIMIT):
    return pltpu.CompilerParams(vmem_limit_bytes=limit)


def in_vmem(count):
    return [pl.BlockSpec(memory_space=pltpu.VMEM)] * count


def measure_kernel(pair, values, stats, held, sems):
    core = lax.axis_index("core")
    steps, rows, _, chans = held.shape
    copies = []
    for step in range(steps):
        at = pl.multiple_of((2 * step + core) * LANES, LANES)
        copies.append(pltpu.make_async_copy(pair.at[:, pl.ds(at, LANES), :], held.at[step], sems.at[step]))
    for copy in copies:
        copy.start()
    for step in range(steps):
        copies[step].wait()
        block = held[step].reshape(rows * LANES, chans).T
        values[step] = block
        block = block.astype(F32)
        mean = jnp.mean(block, axis=0, keepdims=True)
        centred = block - mean
        var = jnp.mean(centred * centred, axis=0, keepdims=True)
        stats[step, 0:1] = mean
        stats[step, 1:2] = lax.rsqrt(var + EPS)


def measure_columns(pair):
    rows, tokens, chans = pair.shape
    steps = tokens // (2 * LANES)
    return pl.pallas_call(
        measure_kernel,
        out_shape=(
            jax.ShapeDtypeStruct((steps, chans, rows * LANES), BF16),
            jax.ShapeDtypeStruct((steps, 2, rows * LANES), F32),
        ),
        in_specs=[pl.BlockSpec(memory_space=pltpu.HBM)],
        out_specs=tuple(in_vmem(2)),
        scratch_shapes=[pltpu.VMEM((steps, rows, LANES, chans), BF16), pltpu.SemaphoreType.DMA((steps,))],
        compiler_params=params(LARGE_LIMIT),
        cost_estimate=pl.CostEstimate(
            flops=6 * steps * rows * LANES * chans,
            bytes_accessed=4 * steps * rows * LANES * chans,
            transcendentals=steps * rows * LANES,
        ),
    )(pair)


def project_kernel(values, stats, gain, bias, mine, theirs, out, own, weights, held):
    core, x = lax.axis_index("core"), lax.axis_index("x")
    weights[:, core] = mine[...]
    weights[:, 1 - core] = theirs[...]
    steps, chans, pairs = values.shape
    slab = 2 * mine.shape[1]
    both = weights[...].reshape(4 * slab, chans)
    gains, biases = gain[...].T, bias[...].T
    for step in range(steps):
        normed = (values[step].astype(F32) - stats[step, 0:1]) * stats[step, 1:2]
        normed = (normed * gains + biases).astype(BF16)
        held[step] = normed
        got = jnp.dot(both, normed, preferred_element_type=F32)

        def gated(first):
            value = jax.nn.sigmoid(got[first : first + slab]) * got[first + slab : first + 2 * slab]
            parts = [value[:, at : at + LANES] for at in range(0, pairs, LANES)]
            return jnp.swapaxes(jnp.stack(parts, axis=0), 0, 1).astype(BF16)

        out[:, step] = gated(0)
        out[:, steps + step] = gated(2 * slab)
    own[...] = held[x]


def project(values, stats, gain, bias, mine, theirs):
    steps, chans, pairs = values.shape
    slab = 2 * mine.shape[1]
    return pl.pallas_call(
        project_kernel,
        out_shape=(
            jax.ShapeDtypeStruct((slab, 2 * steps, pairs // LANES, LANES), BF16),
            jax.ShapeDtypeStruct((chans, pairs), BF16),
        ),
        in_specs=in_vmem(6),
        out_specs=tuple(in_vmem(2)),
        scratch_shapes=[pltpu.VMEM((4, 2) + mine.shape[1:], BF16), pltpu.VMEM(values.shape, BF16)],
        compiler_params=params(),
        cost_estimate=pl.CostEstimate(
            flops=8 * steps * pairs * slab * chans,
            bytes_accessed=4 * steps * pairs * chans,
            transcendentals=2 * steps * pairs * slab,
        ),
    )(values, stats, gain.reshape(1, chans), bias.reshape(1, chans), mine, theirs)


def gate_kernel(normed, weights, out):
    got = lax.dot_general(normed[...], weights[...], OVER_FIRST, preferred_element_type=F32)
    out[...] = jax.nn.sigmoid(got).reshape(out.shape)


def output_gate(normed, weights):
    chans, pairs = normed.shape
    rows = pairs // LANES
    return pl.pallas_call(
        gate_kernel,
        out_shape=jax.ShapeDtypeStruct((rows, LANES, chans), F32),
        in_specs=in_vmem(2),
        out_specs=in_vmem(1)[0],
        compiler_params=params(),
        cost_estimate=pl.CostEstimate(
            flops=2 * pairs * chans * chans, bytes_accessed=6 * pairs * chans, transcendentals=pairs * chans
        ),
    )(normed, weights)


def mirrored(at, size, flip):
    return at + flip * (size - 1 - 2 * at)


def mix_rows(got, left, store):
    sources, parts, rows, _ = got.shape
    blocks = parts // 2

    def joined(ref, start):
        return jnp.concatenate(
            [ref[:, start + at].reshape(sources * rows, LANES) for at in range(blocks)], axis=1
        )

    mixed = lax.dot_general(joined(left, 0), joined(got, blocks), OVER_FIRST, preferred_element_type=F32)
    mixed = mixed.astype(BF16)
    for side in range(blocks):
        for at in range(blocks):
            for y in range(LANES // rows):
                row = side * LANES + y * rows
                store(side, at, y, mixed[row : row + rows, at * LANES : (at + 1) * LANES])


def mix_own_kernel(got, out):
    def store(side, at, y, piece):
        out[y, side, at] = piece

    mix_rows(got, got, store)


def mix_other_kernel(got, other, begun, out):
    core = lax.axis_index("core")
    per, z_count, x_count = out.shape[:3]

    def store_at(z, x, y, piece):
        out[mirrored(y, per, core), mirrored(z, z_count, core), mirrored(x, x_count, core)] = piece

    for y in range(per):
        for side in range(begun.shape[1]):
            for at in range(x_count):
                store_at(2 * side + core, at, y, begun[y, side, at])
    mix_rows(got, other, lambda side, at, y, piece: store_at(2 * side + 1 - core, at, y, piece))


def mix(got, other):
    sources, parts, rows, _ = got.shape
    depth, width = sources * rows, parts // 2 * LANES
    per, blocks = LANES // rows, parts // 2
    cost = pl.CostEstimate(
        flops=2 * depth * width * width, bytes_accessed=2 * (2 * depth * width + width * width), transcendentals=0
    )
    begun = pl.pallas_call(
        mix_own_kernel,
        out_shape=jax.ShapeDtypeStruct((per, blocks, blocks, rows, LANES), BF16),
        in_specs=in_vmem(1),
        out_specs=in_vmem(1)[0],
        compiler_params=params(),
        cost_estimate=cost,
    )(got)
    return pl.pallas_call(
        mix_other_kernel,
        out_shape=jax.ShapeDtypeStruct((per, parts, blocks, rows, LANES), BF16),
        in_specs=in_vmem(3),
        out_specs=in_vmem(1)[0],
        compiler_params=params(),
        cost_estimate=cost,
    )(got, other, begun)


def finish_kernel(mixed, gain, bias, weights, gate, out, held, sems):
    core = lax.axis_index("core")
    _, chans, rows, width = mixed.shape
    places = [mirrored(at, chans, core) for at in range(chans)]
    values = jnp.stack([mixed[0, at].astype(F32) + mixed[1, at].astype(F32) for at in places], axis=0)
    values = values - (jnp.sum(values, axis=0) / chans)[None]
    scale = lax.rsqrt(jnp.sum(values * values, axis=0) / chans + EPS)
    scaled = jnp.swapaxes(values * scale[None], 0, 1)
    scaled = (scaled * gain[...][None] + bias[...][None]).astype(BF16)
    count = held.shape[0]
    step = rows // count
    copies = []
    for piece in range(count):
        at = piece * step
        wide = jnp.concatenate([scaled[at + row] for row in range(step)], axis=1)
        proj = lax.dot_general(wide, weights[...], OVER_FIRST, preferred_element_type=F32)
        held[piece] = (proj.reshape(step, width, -1) * gate[at : at + step]).astype(BF16)
        copies.append(pltpu.make_async_copy(held.at[piece], out.at[pl.ds(at, step)], sems.at[piece]))
        copies[-1].start()
    for copy in copies:
        copy.wait()


def finish(mixed, gain, bias, weights, gate):
    _, _, rows, width = mixed.shape
    chans, outs = weights.shape
    return pl.pallas_call(
        finish_kernel,
        out_shape=jax.ShapeDtypeStruct((rows, width, outs), BF16),
        in_specs=in_vmem(5),
        out_specs=pl.BlockSpec(memory_space=pltpu.HBM),
        scratch_shapes=[pltpu.VMEM((2, rows // 2, width, outs), BF16), pltpu.SemaphoreType.DMA((2,))],
        compiler_params=params(),
        cost_estimate=pl.CostEstimate(
            flops=2 * rows * width * chans * chans, bytes_accessed=10 * chans * rows * width, transcendentals=rows * width
        ),
    )(mixed, gain, bias, weights, gate)


def shards(
    pair,
    ln_gain,
    ln_bias,
    w_a_gate,
    w_a_proj,
    w_b_gate,
    w_b_proj,
    w_gate,
    out_gain,
    out_bias,
    w_out,
):
    rows, _, chans = pair.shape
    depth, x_count = lax.axis_size("row"), lax.axis_size("x")
    half = depth // 2

    mine = jnp.stack([w.T for w in (w_a_gate, w_a_proj, w_b_gate, w_b_proj)])
    theirs = lax.ppermute(mine, "core", SWAP)
    values, stats = measure_columns(pair)
    messages, normed = project(values, stats, ln_gain, ln_bias, mine, theirs)
    shape = messages.shape
    per = LANES // rows
    z_count = depth // per
    halves = [
        [z * per + y for z in range(z_count) for y in range(part * per // 2, (part + 1) * per // 2)] for part in range(2)
    ]
    got = lax.all_to_all(
        messages.reshape(half, -1, LANES), "row", split_axis=0, concat_axis=0, tiled=True, axis_index_groups=halves
    ).reshape(shape)
    got, normed, w_gate, out_gain, out_bias, w_out = lax.optimization_barrier(
        (got, normed, w_gate, out_gain, out_bias, w_out)
    )
    other = lax.ppermute(got[:, : shape[1] // 2], "core", SWAP)
    gate = output_gate(normed, w_gate)

    def in_order(array):
        array = array.reshape(x_count, z_count, per // 2, -1)
        return jnp.transpose(array, (2, 1, 0, 3)).reshape(chans, -1)

    gain = jnp.broadcast_to(in_order(out_gain), (chans, LANES))
    bias = jnp.broadcast_to(in_order(out_bias), (chans, LANES))
    got, gate, gain, bias, out_weights = lax.optimization_barrier((got, gate, gain, bias, in_order(w_out)))

    mixed = mix(got, other).reshape(depth * x_count, rows, LANES)
    group = [x_count * (z * per + y) + x for y in range(per) for z in range(z_count) for x in range(x_count)]
    groups = [[2 * at for at in group], [2 * at + 1 for at in group[::-1]]]
    mixed = lax.all_to_all(
        mixed, ("row", "x", "core"), split_axis=0, concat_axis=0, tiled=True, axis_index_groups=groups
    )
    mixed = mixed.reshape(2, chans, rows, LANES)
    return finish(mixed, gain, bias, out_weights, gate)


def solution(mesh):
    fine = Mesh(mesh.devices.reshape(mesh.devices.shape[0], -1, 2), ("row", "x", "core"))
    chan = ("x", "core")
    in_specs = (
        P("row", None, None),
        P(),
        P(),
        P(None, chan),
        P(None, chan),
        P(None, chan),
        P(None, chan),
        P(),
        P(),
        P(),
        P(),
    )
    return jax.shard_map(shards, mesh=fine, in_specs=in_specs, out_specs=P("row", chan, None), check_vma=False)
```

```python
import jax
import jax.numpy as jnp
from jax import lax
from jax.experimental import pallas as pl
from jax.experimental.pallas import tpu as pltpu
from jax.sharding import Mesh
from jax.sharding import PartitionSpec as P

F32 = jnp.float32
BF16 = jnp.bfloat16
VMEM_LIMIT = 32 * 1024 * 1024
LARGE_LIMIT = 50 * 1024 * 1024
EPS = 1e-05
LANES = 128
SWAP = ((0, 1), (1, 0))
OVER_FIRST = (((0,), (0,)), ((), ()))


def params(limit=VMEM_LIMIT):
    return pltpu.CompilerParams(vmem_limit_bytes=limit)


def in_vmem(count):
    return [pl.BlockSpec(memory_space=pltpu.VMEM)] * count


def mirrored(at, size, flip):
    return at + flip * (size - 1 - 2 * at)


def measure_kernel(pair, values, stats, held, sems):
    core = lax.axis_index("core")
    steps, rows, _, chans = held.shape
    copies = []
    for step in range(steps):
        at = pl.multiple_of((2 * step + core) * LANES, LANES)
        copies.append(pltpu.make_async_copy(pair.at[:, pl.ds(at, LANES), :], held.at[step], sems.at[step]))
    for copy in copies:
        copy.start()
    for step in range(steps):
        copies[step].wait()
        block = held[step].reshape(rows * LANES, chans).T
        values[step] = block
        block = block.astype(F32)
        mean = jnp.mean(block, axis=0, keepdims=True)
        centred = block - mean
        var = jnp.mean(centred * centred, axis=0, keepdims=True)
        stats[step, 0:1] = mean
        stats[step, 1:2] = lax.rsqrt(var + EPS)


def measure_columns(pair):
    rows, tokens, chans = pair.shape
    steps = tokens // (2 * LANES)
    return pl.pallas_call(
        measure_kernel,
        out_shape=(
            jax.ShapeDtypeStruct((steps, chans, rows * LANES), BF16),
            jax.ShapeDtypeStruct((steps, 2, rows * LANES), F32),
        ),
        in_specs=[pl.BlockSpec(memory_space=pltpu.HBM)],
        out_specs=tuple(in_vmem(2)),
        scratch_shapes=[pltpu.VMEM((steps, rows, LANES, chans), BF16), pltpu.SemaphoreType.DMA((steps,))],
        compiler_params=params(LARGE_LIMIT),
        cost_estimate=pl.CostEstimate(
            flops=6 * steps * rows * LANES * chans,
            bytes_accessed=4 * steps * rows * LANES * chans,
            transcendentals=steps * rows * LANES,
        ),
    )(pair)


def project_kernel(values, stats, gain, bias, mine, theirs, out, own, weights, held):
    core, x = lax.axis_index("core"), lax.axis_index("x")
    weights[:, core] = mine[...]
    weights[:, 1 - core] = theirs[...]
    steps, chans, pairs = values.shape
    slab = 2 * mine.shape[1]
    both = weights[...].reshape(4 * slab, chans)
    gains, biases = gain[...].T, bias[...].T
    for step in range(steps):
        normed = (values[step].astype(F32) - stats[step, 0:1]) * stats[step, 1:2]
        normed = (normed * gains + biases).astype(BF16)
        held[step] = normed
        got = jnp.dot(both, normed, preferred_element_type=F32)

        def gated(first):
            value = jax.nn.sigmoid(got[first : first + slab]) * got[first + slab : first + 2 * slab]
            parts = [value[:, at : at + LANES] for at in range(0, pairs, LANES)]
            return jnp.swapaxes(jnp.stack(parts, axis=0), 0, 1).astype(BF16)

        left, right = gated(0), gated(2 * slab)
        for at in range(slab):
            place = mirrored(at, slab, core)
            out[place, step] = left[at]
            out[place, steps + step] = right[at]
    own[...] = held[x]


def project(values, stats, gain, bias, mine, theirs):
    steps, chans, pairs = values.shape
    slab = 2 * mine.shape[1]
    return pl.pallas_call(
        project_kernel,
        out_shape=(
            jax.ShapeDtypeStruct((slab, 2 * steps, pairs // LANES, LANES), BF16),
            jax.ShapeDtypeStruct((chans, pairs), BF16),
        ),
        in_specs=in_vmem(6),
        out_specs=tuple(in_vmem(2)),
        scratch_shapes=[pltpu.VMEM((4, 2) + mine.shape[1:], BF16), pltpu.VMEM(values.shape, BF16)],
        compiler_params=params(),
        cost_estimate=pl.CostEstimate(
            flops=8 * steps * pairs * slab * chans,
            bytes_accessed=4 * steps * pairs * chans,
            transcendentals=2 * steps * pairs * slab,
        ),
    )(values, stats, gain.reshape(1, chans), bias.reshape(1, chans), mine, theirs)


def gate_kernel(normed, weights, out):
    got = lax.dot_general(normed[...], weights[...], OVER_FIRST, preferred_element_type=F32)
    out[...] = jax.nn.sigmoid(got).reshape(out.shape)


def output_gate(normed, weights):
    chans, pairs = normed.shape
    rows = pairs // LANES
    return pl.pallas_call(
        gate_kernel,
        out_shape=jax.ShapeDtypeStruct((rows, LANES, chans), F32),
        in_specs=in_vmem(2),
        out_specs=in_vmem(1)[0],
        compiler_params=params(),
        cost_estimate=pl.CostEstimate(
            flops=2 * pairs * chans * chans, bytes_accessed=6 * pairs * chans, transcendentals=pairs * chans
        ),
    )(normed, weights)


def mix_rows(got, left, backwards, store):
    sources, parts, rows, _ = got.shape
    blocks = parts // 2

    def joined(ref, start, order):
        return jnp.concatenate(
            [jnp.concatenate([ref[source, start + at] for source in order], axis=0) for at in range(blocks)], axis=1
        )

    order = range(sources)
    mixed = lax.dot_general(
        joined(left, 0, order[::-1] if backwards else order),
        joined(got, blocks, order),
        OVER_FIRST,
        preferred_element_type=F32,
    )
    mixed = mixed.astype(BF16)
    for side in range(blocks):
        for at in range(blocks):
            for y in range(LANES // rows):
                row = side * LANES + y * rows
                store(side, at, y, mixed[row : row + rows, at * LANES : (at + 1) * LANES])


def mix_own_kernel(got, out):
    def store(side, at, y, piece):
        out[y, side, at] = piece

    mix_rows(got, got, False, store)


def mix_other_kernel(got, other, begun, out):
    core = lax.axis_index("core")
    per, z_count, x_count = out.shape[:3]

    def store_at(z, x, y, piece):
        out[mirrored(y, per, core), mirrored(z, z_count, core), mirrored(x, x_count, core)] = piece

    for y in range(per):
        for side in range(begun.shape[1]):
            for at in range(x_count):
                store_at(2 * side + core, at, y, begun[y, side, at])
    mix_rows(got, other, True, lambda side, at, y, piece: store_at(2 * side + 1 - core, at, y, piece))


def mix(got, other):
    sources, parts, rows, _ = got.shape
    depth, width = sources * rows, parts // 2 * LANES
    per, blocks = LANES // rows, parts // 2
    cost = pl.CostEstimate(
        flops=2 * depth * width * width, bytes_accessed=2 * (2 * depth * width + width * width), transcendentals=0
    )
    begun = pl.pallas_call(
        mix_own_kernel,
        out_shape=jax.ShapeDtypeStruct((per, blocks, blocks, rows, LANES), BF16),
        in_specs=in_vmem(1),
        out_specs=in_vmem(1)[0],
        compiler_params=params(),
        cost_estimate=cost,
    )(got)
    return pl.pallas_call(
        mix_other_kernel,
        out_shape=jax.ShapeDtypeStruct((per, parts, blocks, rows, LANES), BF16),
        in_specs=in_vmem(3),
        out_specs=in_vmem(1)[0],
        compiler_params=params(),
        cost_estimate=cost,
    )(got, other, begun)


def finish_kernel(mixed, gain, bias, weights, gate, out, held, sems):
    core = lax.axis_index("core")
    _, chans, rows, width = mixed.shape
    places = [mirrored(at, chans, core) for at in range(chans)]
    values = jnp.stack([mixed[0, at].astype(F32) + mixed[1, at].astype(F32) for at in places], axis=0)
    values = values - (jnp.sum(values, axis=0) / chans)[None]
    scale = lax.rsqrt(jnp.sum(values * values, axis=0) / chans + EPS)
    scaled = jnp.swapaxes(values * scale[None], 0, 1)
    scaled = (scaled * gain[...][None] + bias[...][None]).astype(BF16)
    count = held.shape[0]
    step = rows // count
    copies = []
    for piece in range(count):
        at = piece * step
        wide = jnp.concatenate([scaled[at + row] for row in range(step)], axis=1)
        proj = lax.dot_general(wide, weights[...], OVER_FIRST, preferred_element_type=F32)
        held[piece] = (proj.reshape(step, width, -1) * gate[at : at + step]).astype(BF16)
        copies.append(pltpu.make_async_copy(held.at[piece], out.at[pl.ds(at, step)], sems.at[piece]))
        copies[-1].start()
    for copy in copies:
        copy.wait()


def finish(mixed, gain, bias, weights, gate):
    _, _, rows, width = mixed.shape
    chans, outs = weights.shape
    return pl.pallas_call(
        finish_kernel,
        out_shape=jax.ShapeDtypeStruct((rows, width, outs), BF16),
        in_specs=in_vmem(5),
        out_specs=pl.BlockSpec(memory_space=pltpu.HBM),
        scratch_shapes=[pltpu.VMEM((2, rows // 2, width, outs), BF16), pltpu.SemaphoreType.DMA((2,))],
        compiler_params=params(),
        cost_estimate=pl.CostEstimate(
            flops=2 * rows * width * chans * chans, bytes_accessed=10 * chans * rows * width, transcendentals=rows * width
        ),
    )(mixed, gain, bias, weights, gate)


def shards(
    pair,
    ln_gain,
    ln_bias,
    w_a_gate,
    w_a_proj,
    w_b_gate,
    w_b_proj,
    w_gate,
    out_gain,
    out_bias,
    w_out,
):
    rows, _, chans = pair.shape
    depth, x_count = lax.axis_size("row"), lax.axis_size("x")
    half = depth // 2

    mine = jnp.stack([w.T for w in (w_a_gate, w_a_proj, w_b_gate, w_b_proj)])
    theirs = lax.ppermute(mine, "core", SWAP)
    values, stats = measure_columns(pair)
    messages, normed = project(values, stats, ln_gain, ln_bias, mine, theirs)
    shape = messages.shape
    per = LANES // rows
    z_count = depth // per
    halves = [
        [z * per + y for z in range(z_count) for y in range(part * per // 2, (part + 1) * per // 2)] for part in range(2)
    ]
    groups = [[2 * at for at in part] for part in halves] + [[2 * at + 1 for at in part[::-1]] for part in halves]
    got = lax.all_to_all(
        messages.reshape(half, -1, LANES),
        ("row", "core"),
        split_axis=0,
        concat_axis=0,
        tiled=True,
        axis_index_groups=groups,
    ).reshape(shape)
    got, normed, w_gate, out_gain, out_bias, w_out = lax.optimization_barrier(
        (got, normed, w_gate, out_gain, out_bias, w_out)
    )
    other = lax.ppermute(got[:, : shape[1] // 2], "core", SWAP)
    gate = output_gate(normed, w_gate)

    def in_order(array):
        array = array.reshape(x_count, z_count, per // 2, -1)
        return jnp.transpose(array, (2, 1, 0, 3)).reshape(chans, -1)

    gain = jnp.broadcast_to(in_order(out_gain), (chans, LANES))
    bias = jnp.broadcast_to(in_order(out_bias), (chans, LANES))
    got, gate, gain, bias, out_weights = lax.optimization_barrier((got, gate, gain, bias, in_order(w_out)))

    mixed = mix(got, other).reshape(depth * x_count, rows, LANES)
    group = [x_count * (z * per + y) + x for y in range(per) for z in range(z_count) for x in range(x_count)]
    groups = [[2 * at for at in group], [2 * at + 1 for at in group[::-1]]]
    mixed = lax.all_to_all(
        mixed, ("row", "x", "core"), split_axis=0, concat_axis=0, tiled=True, axis_index_groups=groups
    )
    mixed = mixed.reshape(2, chans, rows, LANES)
    return finish(mixed, gain, bias, out_weights, gate)


def solution(mesh):
    fine = Mesh(mesh.devices.reshape(mesh.devices.shape[0], -1, 2), ("row", "x", "core"))
    chan = ("x", "core")
    in_specs = (
        P("row", None, None),
        P(),
        P(),
        P(None, chan),
        P(None, chan),
        P(None, chan),
        P(None, chan),
        P(),
        P(),
        P(),
        P(),
    )
    return jax.shard_map(shards, mesh=fine, in_specs=in_specs, out_specs=P("row", chan, None), check_vma=False)
```

```python
import jax
import jax.numpy as jnp
from jax import lax
from jax.experimental import pallas as pl
from jax.experimental.pallas import tpu as pltpu
from jax.sharding import Mesh
from jax.sharding import PartitionSpec as P

F32 = jnp.float32
BF16 = jnp.bfloat16
VMEM_LIMIT = 32 * 1024 * 1024
LARGE_LIMIT = 50 * 1024 * 1024
EPS = 1e-05
LANES = 128
SWAP = ((0, 1), (1, 0))
OVER_FIRST = (((0,), (0,)), ((), ()))


def params(limit=VMEM_LIMIT):
    return pltpu.CompilerParams(vmem_limit_bytes=limit)


def in_vmem(count):
    return [pl.BlockSpec(memory_space=pltpu.VMEM)] * count


def mirrored(at, size, flip):
    return at + flip * (size - 1 - 2 * at)


def measure_kernel(pair, values, stats, held, sems):
    core = lax.axis_index("core")
    steps, rows, _, chans = held.shape
    copies = []
    for step in range(steps):
        at = pl.multiple_of((2 * step + core) * LANES, LANES)
        copies.append(pltpu.make_async_copy(pair.at[:, pl.ds(at, LANES), :], held.at[step], sems.at[step]))
    for copy in copies:
        copy.start()
    for step in range(steps):
        copies[step].wait()
        block = held[step].reshape(rows * LANES, chans).T
        values[step] = block
        block = block.astype(F32)
        mean = jnp.mean(block, axis=0, keepdims=True)
        centred = block - mean
        var = jnp.mean(centred * centred, axis=0, keepdims=True)
        stats[step, 0:1] = mean
        stats[step, 1:2] = lax.rsqrt(var + EPS)


def measure_columns(pair):
    rows, tokens, chans = pair.shape
    steps = tokens // (2 * LANES)
    return pl.pallas_call(
        measure_kernel,
        out_shape=(
            jax.ShapeDtypeStruct((steps, chans, rows * LANES), BF16),
            jax.ShapeDtypeStruct((steps, 2, rows * LANES), F32),
        ),
        in_specs=[pl.BlockSpec(memory_space=pltpu.HBM)],
        out_specs=tuple(in_vmem(2)),
        scratch_shapes=[pltpu.VMEM((steps, rows, LANES, chans), BF16), pltpu.SemaphoreType.DMA((steps,))],
        compiler_params=params(LARGE_LIMIT),
        cost_estimate=pl.CostEstimate(
            flops=6 * steps * rows * LANES * chans,
            bytes_accessed=4 * steps * rows * LANES * chans,
            transcendentals=steps * rows * LANES,
        ),
    )(pair)


def project_kernel(values, stats, gain, bias, mine, theirs, out, own, weights, held):
    core, x = lax.axis_index("core"), lax.axis_index("x")
    weights[:, core] = mine[...]
    weights[:, 1 - core] = theirs[...]
    steps, chans, pairs = values.shape
    slab = 2 * mine.shape[1]
    both = weights[...].reshape(4 * slab, chans)
    gains, biases = gain[...].T, bias[...].T
    for step in range(steps):
        normed = (values[step].astype(F32) - stats[step, 0:1]) * stats[step, 1:2]
        normed = (normed * gains + biases).astype(BF16)
        held[step] = normed
        got = jnp.dot(both, normed, preferred_element_type=F32)

        def gated(first):
            value = jax.nn.sigmoid(got[first : first + slab]) * got[first + slab : first + 2 * slab]
            parts = [value[:, at : at + LANES] for at in range(0, pairs, LANES)]
            return jnp.swapaxes(jnp.stack(parts, axis=0), 0, 1).astype(BF16)

        left, right = gated(0), gated(2 * slab)
        for at in range(slab):
            place = mirrored(at, slab, core)
            out[place, step] = left[at]
            out[place, steps + step] = right[at]
    own[...] = held[x]


def project(values, stats, gain, bias, mine, theirs):
    steps, chans, pairs = values.shape
    slab = 2 * mine.shape[1]
    return pl.pallas_call(
        project_kernel,
        out_shape=(
            jax.ShapeDtypeStruct((slab, 2 * steps, pairs // LANES, LANES), BF16),
            jax.ShapeDtypeStruct((chans, pairs), BF16),
        ),
        in_specs=in_vmem(6),
        out_specs=tuple(in_vmem(2)),
        scratch_shapes=[pltpu.VMEM((4, 2) + mine.shape[1:], BF16), pltpu.VMEM(values.shape, BF16)],
        compiler_params=params(),
        cost_estimate=pl.CostEstimate(
            flops=8 * steps * pairs * slab * chans,
            bytes_accessed=4 * steps * pairs * chans,
            transcendentals=2 * steps * pairs * slab,
        ),
    )(values, stats, gain.reshape(1, chans), bias.reshape(1, chans), mine, theirs)


def gate_kernel(normed, weights, out):
    got = lax.dot_general(normed[...], weights[...], OVER_FIRST, preferred_element_type=F32)
    out[...] = jax.nn.sigmoid(got).reshape(out.shape)


def output_gate(normed, weights):
    chans, pairs = normed.shape
    rows = pairs // LANES
    return pl.pallas_call(
        gate_kernel,
        out_shape=jax.ShapeDtypeStruct((rows, LANES, chans), F32),
        in_specs=in_vmem(2),
        out_specs=in_vmem(1)[0],
        compiler_params=params(),
        cost_estimate=pl.CostEstimate(
            flops=2 * pairs * chans * chans, bytes_accessed=6 * pairs * chans, transcendentals=pairs * chans
        ),
    )(normed, weights)


def mix_rows(got, left, backwards, store):
    sources, parts, rows, _ = got.shape
    blocks = parts // 2

    def joined(ref, start, order):
        return jnp.concatenate(
            [jnp.concatenate([ref[source, start + at] for source in order], axis=0) for at in range(blocks)], axis=1
        )

    order = range(sources)
    mixed = lax.dot_general(
        joined(left, 0, order[::-1] if backwards else order),
        joined(got, blocks, order),
        OVER_FIRST,
        preferred_element_type=F32,
    )
    mixed = mixed.astype(BF16)
    for side in range(blocks):
        for at in range(blocks):
            for y in range(LANES // rows):
                row = side * LANES + y * rows
                store(side, at, y, mixed[row : row + rows, at * LANES : (at + 1) * LANES])


def mix_own_kernel(got, out):
    def store(side, at, y, piece):
        out[y, side, at] = piece

    mix_rows(got, got, False, store)


def mix_other_kernel(got, other, begun, out):
    core = lax.axis_index("core")
    per, z_count, x_count = out.shape[:3]

    def store_at(z, x, y, piece):
        out[mirrored(y, per, core), mirrored(z, z_count, core), mirrored(x, x_count, core)] = piece

    for y in range(per):
        for side in range(begun.shape[1]):
            for at in range(x_count):
                store_at(2 * side + core, at, y, begun[y, side, at])
    mix_rows(got, other, True, lambda side, at, y, piece: store_at(2 * side + 1 - core, at, y, piece))


def mix(got, other):
    sources, parts, rows, _ = got.shape
    depth, width = sources * rows, parts // 2 * LANES
    per, blocks = LANES // rows, parts // 2
    cost = pl.CostEstimate(
        flops=2 * depth * width * width, bytes_accessed=2 * (2 * depth * width + width * width), transcendentals=0
    )
    begun = pl.pallas_call(
        mix_own_kernel,
        out_shape=jax.ShapeDtypeStruct((per, blocks, blocks, rows, LANES), BF16),
        in_specs=in_vmem(1),
        out_specs=in_vmem(1)[0],
        compiler_params=params(),
        cost_estimate=cost,
    )(got)
    return pl.pallas_call(
        mix_other_kernel,
        out_shape=jax.ShapeDtypeStruct((per, parts, blocks, rows, LANES), BF16),
        in_specs=in_vmem(3),
        out_specs=in_vmem(1)[0],
        compiler_params=params(),
        cost_estimate=cost,
    )(got, other, begun)


def finish_kernel(mixed, gain, bias, weights, gate, out, held, sems):
    core = lax.axis_index("core")
    _, chans, rows, width = mixed.shape
    places = [mirrored(at, chans, core) for at in range(chans)]
    values = jnp.stack([mixed[0, at].astype(F32) + mixed[1, at].astype(F32) for at in places], axis=0)
    values = values - (jnp.sum(values, axis=0) / chans)[None]
    scale = lax.rsqrt(jnp.sum(values * values, axis=0) / chans + EPS)
    scaled = jnp.swapaxes(values * scale[None], 0, 1)
    scaled = (scaled * gain[...][None] + bias[...][None]).astype(BF16)
    count = held.shape[0]
    step = rows // count
    copies = []
    for piece in range(count):
        at = piece * step
        wide = jnp.concatenate([scaled[at + row] for row in range(step)], axis=1)
        proj = lax.dot_general(wide, weights[...], OVER_FIRST, preferred_element_type=F32)
        held[piece] = (proj.reshape(step, width, -1) * gate[at : at + step]).astype(BF16)
        copies.append(pltpu.make_async_copy(held.at[piece], out.at[pl.ds(at, step)], sems.at[piece]))
        copies[-1].start()
    for copy in copies:
        copy.wait()


def finish(mixed, gain, bias, weights, gate):
    _, _, rows, width = mixed.shape
    chans, outs = weights.shape
    return pl.pallas_call(
        finish_kernel,
        out_shape=jax.ShapeDtypeStruct((rows, width, outs), BF16),
        in_specs=in_vmem(5),
        out_specs=pl.BlockSpec(memory_space=pltpu.HBM),
        scratch_shapes=[pltpu.VMEM((2, rows // 2, width, outs), BF16), pltpu.SemaphoreType.DMA((2,))],
        compiler_params=params(),
        cost_estimate=pl.CostEstimate(
            flops=2 * rows * width * chans * chans, bytes_accessed=10 * chans * rows * width, transcendentals=rows * width
        ),
    )(mixed, gain, bias, weights, gate)


def shards(
    pair,
    ln_gain,
    ln_bias,
    w_a_gate,
    w_a_proj,
    w_b_gate,
    w_b_proj,
    w_gate,
    out_gain,
    out_bias,
    w_out,
):
    rows, _, chans = pair.shape
    depth, x_count = lax.axis_size("row"), lax.axis_size("x")
    half = depth // 2

    mine = jnp.stack([w.T for w in (w_a_gate, w_a_proj, w_b_gate, w_b_proj)])
    theirs = lax.ppermute(mine, "core", SWAP)
    values, stats = measure_columns(pair)
    messages, normed = project(values, stats, ln_gain, ln_bias, mine, theirs)
    shape = messages.shape
    per = LANES // rows
    z_count = depth // per
    halves = [
        [z * per + y for y in range(part * per // 2, (part + 1) * per // 2) for z in range(z_count)] for part in range(2)
    ]
    groups = [[2 * at for at in part] for part in halves] + [[2 * at + 1 for at in part[::-1]] for part in halves]
    got = lax.all_to_all(
        messages.reshape(half, -1, LANES),
        ("row", "core"),
        split_axis=0,
        concat_axis=0,
        tiled=True,
        axis_index_groups=groups,
    ).reshape(shape)
    got, normed, w_gate, out_gain, out_bias, w_out = lax.optimization_barrier(
        (got, normed, w_gate, out_gain, out_bias, w_out)
    )
    other = lax.ppermute(got[:, : shape[1] // 2], "core", SWAP)
    gate = output_gate(normed, w_gate)

    def in_order(array):
        array = array.reshape(x_count, half, -1)
        return jnp.swapaxes(array, 0, 1).reshape(chans, -1)

    gain = jnp.broadcast_to(in_order(out_gain), (chans, LANES))
    bias = jnp.broadcast_to(in_order(out_bias), (chans, LANES))
    got, gate, gain, bias, out_weights = lax.optimization_barrier((got, gate, gain, bias, in_order(w_out)))

    mixed = mix(got, other).reshape(depth * x_count, rows, LANES)
    group = [x_count * (z * per + y) + x for y in range(per) for z in range(z_count) for x in range(x_count)]
    groups = [[2 * at for at in group], [2 * at + 1 for at in group[::-1]]]
    mixed = lax.all_to_all(
        mixed, ("row", "x", "core"), split_axis=0, concat_axis=0, tiled=True, axis_index_groups=groups
    )
    mixed = mixed.reshape(2, chans, rows, LANES)
    return finish(mixed, gain, bias, out_weights, gate)


def solution(mesh):
    fine = Mesh(mesh.devices.reshape(mesh.devices.shape[0], -1, 2), ("row", "x", "core"))
    chan = ("x", "core")
    in_specs = (
        P("row", None, None),
        P(),
        P(),
        P(None, chan),
        P(None, chan),
        P(None, chan),
        P(None, chan),
        P(),
        P(),
        P(),
        P(),
    )
    return jax.shard_map(shards, mesh=fine, in_specs=in_specs, out_specs=P("row", chan, None), check_vma=False)
```

```python
import jax
import jax.numpy as jnp
from jax import lax
from jax.experimental import pallas as pl
from jax.experimental.pallas import tpu as pltpu
from jax.sharding import Mesh
from jax.sharding import PartitionSpec as P

F32 = jnp.float32
BF16 = jnp.bfloat16
VMEM_LIMIT = 32 * 1024 * 1024
LARGE_LIMIT = 50 * 1024 * 1024
EPS = 1e-05
LANES = 128
SWAP = ((0, 1), (1, 0))
OVER_FIRST = (((0,), (0,)), ((), ()))


def params(limit=VMEM_LIMIT):
    return pltpu.CompilerParams(vmem_limit_bytes=limit)


def in_vmem(count):
    return [pl.BlockSpec(memory_space=pltpu.VMEM)] * count


def mirrored(at, size, flip):
    return at + flip * (size - 1 - 2 * at)


def measure_kernel(pair, values, stats, held, sems):
    core = lax.axis_index("core")
    steps, rows, _, chans = held.shape
    copies = []
    for step in range(steps):
        at = pl.multiple_of((2 * step + core) * LANES, LANES)
        copies.append(pltpu.make_async_copy(pair.at[:, pl.ds(at, LANES), :], held.at[step], sems.at[step]))
    for copy in copies:
        copy.start()
    for step in range(steps):
        copies[step].wait()
        block = held[step].reshape(rows * LANES, chans).T
        values[step] = block
        block = block.astype(F32)
        mean = jnp.mean(block, axis=0, keepdims=True)
        centred = block - mean
        var = jnp.mean(centred * centred, axis=0, keepdims=True)
        stats[step, 0:1] = mean
        stats[step, 1:2] = lax.rsqrt(var + EPS)


def measure_columns(pair):
    rows, tokens, chans = pair.shape
    steps = tokens // (2 * LANES)
    return pl.pallas_call(
        measure_kernel,
        out_shape=(
            jax.ShapeDtypeStruct((steps, chans, rows * LANES), BF16),
            jax.ShapeDtypeStruct((steps, 2, rows * LANES), F32),
        ),
        in_specs=[pl.BlockSpec(memory_space=pltpu.HBM)],
        out_specs=tuple(in_vmem(2)),
        scratch_shapes=[pltpu.VMEM((steps, rows, LANES, chans), BF16), pltpu.SemaphoreType.DMA((steps,))],
        compiler_params=params(LARGE_LIMIT),
        cost_estimate=pl.CostEstimate(
            flops=6 * steps * rows * LANES * chans,
            bytes_accessed=4 * steps * rows * LANES * chans,
            transcendentals=steps * rows * LANES,
        ),
    )(pair)


def project_kernel(values, stats, gain, bias, mine, theirs, out, own, weights, held):
    core, x = lax.axis_index("core"), lax.axis_index("x")
    weights[:, core] = mine[...]
    weights[:, 1 - core] = theirs[...]
    steps, chans, pairs = values.shape
    slab = 2 * mine.shape[1]
    both = weights[...].reshape(4 * slab, chans)
    gains, biases = gain[...].T, bias[...].T
    for step in range(steps):
        normed = (values[step].astype(F32) - stats[step, 0:1]) * stats[step, 1:2]
        normed = (normed * gains + biases).astype(BF16)
        held[step] = normed
        got = jnp.dot(both, normed, preferred_element_type=F32)

        def gated(first):
            value = jax.nn.sigmoid(got[first : first + slab]) * got[first + slab : first + 2 * slab]
            parts = [value[:, at : at + LANES] for at in range(0, pairs, LANES)]
            return jnp.swapaxes(jnp.stack(parts, axis=0), 0, 1).astype(BF16)

        left, right = gated(0), gated(2 * slab)
        for at in range(slab):
            place = mirrored(at, slab, core)
            out[place, step] = left[at]
            out[place, steps + step] = right[at]
    own[...] = held[x]


def project(values, stats, gain, bias, mine, theirs):
    steps, chans, pairs = values.shape
    slab = 2 * mine.shape[1]
    return pl.pallas_call(
        project_kernel,
        out_shape=(
            jax.ShapeDtypeStruct((slab, 2 * steps, pairs // LANES, LANES), BF16),
            jax.ShapeDtypeStruct((chans, pairs), BF16),
        ),
        in_specs=in_vmem(6),
        out_specs=tuple(in_vmem(2)),
        scratch_shapes=[pltpu.VMEM((4, 2) + mine.shape[1:], BF16), pltpu.VMEM(values.shape, BF16)],
        compiler_params=params(),
        cost_estimate=pl.CostEstimate(
            flops=8 * steps * pairs * slab * chans,
            bytes_accessed=4 * steps * pairs * chans,
            transcendentals=2 * steps * pairs * slab,
        ),
    )(values, stats, gain.reshape(1, chans), bias.reshape(1, chans), mine, theirs)


def gate_kernel(normed, weights, out):
    got = lax.dot_general(normed[...], weights[...], OVER_FIRST, preferred_element_type=F32)
    out[...] = jax.nn.sigmoid(got).reshape(out.shape)


def output_gate(normed, weights):
    chans, pairs = normed.shape
    rows = pairs // LANES
    return pl.pallas_call(
        gate_kernel,
        out_shape=jax.ShapeDtypeStruct((rows, LANES, chans), F32),
        in_specs=in_vmem(2),
        out_specs=in_vmem(1)[0],
        compiler_params=params(),
        cost_estimate=pl.CostEstimate(
            flops=2 * pairs * chans * chans, bytes_accessed=6 * pairs * chans, transcendentals=pairs * chans
        ),
    )(normed, weights)


def mix_rows(got, left, backwards, store):
    sources, parts, rows, _ = got.shape
    blocks = parts // 2

    def joined(ref, start, order):
        return jnp.concatenate(
            [jnp.concatenate([ref[source, start + at] for source in order], axis=0) for at in range(blocks)], axis=1
        )

    order = range(sources)
    mixed = lax.dot_general(
        joined(left, 0, order[::-1] if backwards else order),
        joined(got, blocks, order),
        OVER_FIRST,
        preferred_element_type=F32,
    )
    mixed = mixed.astype(BF16)
    for side in range(blocks):
        for at in range(blocks):
            for y in range(LANES // rows):
                row = side * LANES + y * rows
                store(side, at, y, mixed[row : row + rows, at * LANES : (at + 1) * LANES])


def mix_own_kernel(got, out):
    def store(side, at, y, piece):
        out[y, side, at] = piece

    mix_rows(got, got, False, store)


def mix_other_kernel(got, other, begun, out):
    core = lax.axis_index("core")
    per, z_count, x_count = out.shape[:3]

    def store_at(z, x, y, piece):
        out[mirrored(y, per, core), mirrored(z, z_count, core), mirrored(x, x_count, core)] = piece

    for y in range(per):
        for side in range(begun.shape[1]):
            for at in range(x_count):
                store_at(2 * side + core, at, y, begun[y, side, at])
    mix_rows(got, other, True, lambda side, at, y, piece: store_at(2 * side + 1 - core, at, y, piece))


def mix(got, other):
    sources, parts, rows, _ = got.shape
    depth, width = sources * rows, parts // 2 * LANES
    per, blocks = LANES // rows, parts // 2
    cost = pl.CostEstimate(
        flops=2 * depth * width * width, bytes_accessed=2 * (2 * depth * width + width * width), transcendentals=0
    )
    begun = pl.pallas_call(
        mix_own_kernel,
        out_shape=jax.ShapeDtypeStruct((per, blocks, blocks, rows, LANES), BF16),
        in_specs=in_vmem(1),
        out_specs=in_vmem(1)[0],
        compiler_params=params(),
        cost_estimate=cost,
    )(got)
    return pl.pallas_call(
        mix_other_kernel,
        out_shape=jax.ShapeDtypeStruct((per, parts, blocks, rows, LANES), BF16),
        in_specs=in_vmem(3),
        out_specs=in_vmem(1)[0],
        compiler_params=params(),
        cost_estimate=cost,
    )(got, other, begun)


def finish_kernel(mixed, gain, bias, weights, gate, out, held, sems):
    core = lax.axis_index("core")
    _, chans, rows, width = mixed.shape
    places = [mirrored(at, chans, core) for at in range(chans)]
    values = jnp.stack([mixed[0, at].astype(F32) + mixed[1, at].astype(F32) for at in places], axis=0)
    values = jnp.swapaxes(values, 0, 1)
    values = values - jnp.mean(values, axis=1, keepdims=True)
    scale = lax.rsqrt(jnp.mean(values * values, axis=1, keepdims=True) + EPS)
    scaled = (values * scale * gain[...][None] + bias[...][None]).astype(BF16)
    count = held.shape[0]
    step = rows // count
    copies = []
    for piece in range(count):
        at = piece * step
        wide = jnp.concatenate([scaled[at + row] for row in range(step)], axis=1)
        proj = lax.dot_general(wide, weights[...], OVER_FIRST, preferred_element_type=F32)
        held[piece] = (proj.reshape(step, width, -1) * gate[at : at + step]).astype(BF16)
        copies.append(pltpu.make_async_copy(held.at[piece], out.at[pl.ds(at, step)], sems.at[piece]))
        copies[-1].start()
    for copy in copies:
        copy.wait()


def finish(mixed, gain, bias, weights, gate):
    _, _, rows, width = mixed.shape
    chans, outs = weights.shape
    return pl.pallas_call(
        finish_kernel,
        out_shape=jax.ShapeDtypeStruct((rows, width, outs), BF16),
        in_specs=in_vmem(5),
        out_specs=pl.BlockSpec(memory_space=pltpu.HBM),
        scratch_shapes=[pltpu.VMEM((2, rows // 2, width, outs), BF16), pltpu.SemaphoreType.DMA((2,))],
        compiler_params=params(),
        cost_estimate=pl.CostEstimate(
            flops=2 * rows * width * chans * chans, bytes_accessed=10 * chans * rows * width, transcendentals=rows * width
        ),
    )(mixed, gain, bias, weights, gate)


def shards(
    pair,
    ln_gain,
    ln_bias,
    w_a_gate,
    w_a_proj,
    w_b_gate,
    w_b_proj,
    w_gate,
    out_gain,
    out_bias,
    w_out,
):
    rows, _, chans = pair.shape
    depth, x_count = lax.axis_size("row"), lax.axis_size("x")
    half = depth // 2

    mine = jnp.stack([w.T for w in (w_a_gate, w_a_proj, w_b_gate, w_b_proj)])
    theirs = lax.ppermute(mine, "core", SWAP)
    values, stats = measure_columns(pair)
    messages, normed = project(values, stats, ln_gain, ln_bias, mine, theirs)
    shape = messages.shape
    per = LANES // rows
    z_count = depth // per
    halves = [
        [z * per + y for y in range(part * per // 2, (part + 1) * per // 2) for z in range(z_count)] for part in range(2)
    ]
    groups = [[2 * at for at in part] for part in halves] + [[2 * at + 1 for at in part[::-1]] for part in halves]
    got = lax.all_to_all(
        messages.reshape(half, -1, LANES),
        ("row", "core"),
        split_axis=0,
        concat_axis=0,
        tiled=True,
        axis_index_groups=groups,
    ).reshape(shape)
    got, normed, w_gate, out_gain, out_bias, w_out = lax.optimization_barrier(
        (got, normed, w_gate, out_gain, out_bias, w_out)
    )
    other = lax.ppermute(got[:, : shape[1] // 2], "core", SWAP)
    gate = output_gate(normed, w_gate)

    def in_order(array):
        array = array.reshape(x_count, half, -1)
        return jnp.swapaxes(array, 0, 1).reshape(chans, -1)

    gain = jnp.broadcast_to(in_order(out_gain), (chans, LANES))
    bias = jnp.broadcast_to(in_order(out_bias), (chans, LANES))
    got, gate, gain, bias, out_weights = lax.optimization_barrier((got, gate, gain, bias, in_order(w_out)))

    mixed = mix(got, other).reshape(depth * x_count, rows, LANES)
    group = [x_count * (z * per + y) + x for y in range(per) for z in range(z_count) for x in range(x_count)]
    groups = [[2 * at for at in group], [2 * at + 1 for at in group[::-1]]]
    mixed = lax.all_to_all(
        mixed, ("row", "x", "core"), split_axis=0, concat_axis=0, tiled=True, axis_index_groups=groups
    )
    mixed = mixed.reshape(2, chans, rows, LANES)
    return finish(mixed, gain, bias, out_weights, gate)


def solution(mesh):
    fine = Mesh(mesh.devices.reshape(mesh.devices.shape[0], -1, 2), ("row", "x", "core"))
    chan = ("x", "core")
    in_specs = (
        P("row", None, None),
        P(),
        P(),
        P(None, chan),
        P(None, chan),
        P(None, chan),
        P(None, chan),
        P(),
        P(),
        P(),
        P(),
    )
    return jax.shard_map(shards, mesh=fine, in_specs=in_specs, out_specs=P("row", chan, None), check_vma=False)
```
